256 devices in a mesh: band: 8 (over y, core), pw: 32 (over z, x).
Axes of the slice: x: 4, y: 4, z: 8, core: 2. Of those that a mesh axis runs over, the one named last changes fastest.
Arguments:
- orbitals: float32 [2, 8, 360, 4096], P(None, 'band', None, 'pw'), may hold values from -6 to 6
- response: float32 [2, 8, 360, 4096], P(None, 'band', None, 'pw'), may hold values from -6 to 6
- potential: float32 [32, 360, 360], P('pw'), may hold values from -8 to 8
- perturbation: float32 [32, 360, 360], P('pw'), may hold values from -6 to 6
- energies: float32 [8], P('band'), may hold values from -1 to 0
- stick_pos: int32 [4096], P('pw'), may hold values from 0 to 129599, as said below
Outputs:
- residual: float32 [2, 8, 360, 4096], P(None, 'band', None, 'pw')
- density: float32 [32, 360, 360], P('pw', 'band')
The draws below stay inside these ranges and needn't reach their ends.
Inputs may be any that keep to these rules, and one draw needn't show every extreme that they name: `stick_pos`: the 4096 positions are all different; 0 and 129599 are among them.
All inputs are finite; a program needn't handle non-finite values.
Results may differ from the reference program's by a relative error of at most 0.0003.
Values sent between devices are 32-bit elements; how exact they have to be, the bound alone decides.
No kernel may reach another device: no remote copies, remote signals or barrier semaphores. Data moves between devices by JAX's collectives and lax.ppermute only.
A program may use at most 64 MiB of HBM per device.

```python
import math
import jax
import jax.numpy as jnp
from jax import lax

GRID = 360
NBANDS = 8
STICKS = 4096
SL = 32


def draw_stick_pos(key, part):
    key = jax.random.fold_in(key, 11)
    inner = jax.random.permutation(key, GRID * GRID - 2)[:STICKS - 2] + 1
    chosen = jnp.concatenate([jnp.array([0, GRID * GRID - 1], jnp.int32), inner.astype(jnp.int32)])
    shuffle = jax.random.permutation(jax.random.fold_in(key, 5), STICKS)
    return chosen[shuffle].astype(jnp.int32)


def levels(rng, dims, pieces, low, top_value):
    loudness, own = 1.0, jax.random.fold_in(rng, 6)
    for axis_at, blocks in pieces:
        draws = jnp.exp(jax.random.uniform(jax.random.fold_in(own, axis_at), (blocks,), jnp.float32, low / len(pieces), top_value / len(pieces)))
        loudness = loudness * jnp.repeat(draws, dims[axis_at] // blocks).reshape([-1 if axis == axis_at else 1 for axis in range(len(dims))])
    return loudness


def scatter_about(rng, dims, scale, reach, shards=(), kind=jnp.bfloat16):
    drawn = scale * jax.random.normal(rng, dims, jnp.float32)
    if shards:
        drawn = drawn * levels(rng, dims, shards, -0.22, 0.18)
    return jnp.clip(drawn, -reach, reach).astype(kind)


def setup_inputs(seed: int = 0) -> dict:
    streams_of = jax.random.split(jax.random.key(seed), 7)
    return {
        "orbitals": scatter_about(streams_of[0], (2, NBANDS, GRID, STICKS), 1.0, 6.0, ((1, 8), (3, 32)), jnp.float32),
        "response": scatter_about(streams_of[1], (2, NBANDS, GRID, STICKS), 1.0, 6.0, ((1, 8), (3, 32)), jnp.float32),
        "potential": scatter_about(streams_of[2], (SL, GRID, GRID), 1.5, 8.0, ((0, 32),), jnp.float32),
        "perturbation": scatter_about(streams_of[3], (SL, GRID, GRID), 1.0, 6.0, ((0, 32),), jnp.float32),
        "energies": jnp.clip(-1.0 + 1.0 * jax.random.uniform(streams_of[4], (NBANDS,), jnp.float32) ** levels(streams_of[4], (NBANDS,), ((0, 8),), -0.2, 0.2), -1.0, 0.0),
        "stick_pos": draw_stick_pos(jax.random.fold_in(streams_of[6], 71), 0),
    }


HIGHEST = lax.Precision.HIGHEST

def phase_tables(rows, cols, length):
    left = jnp.arange(rows, dtype=jnp.int32)[:, None]
    right = jnp.arange(cols, dtype=jnp.int32)[None, :]
    turns = (left * right % length).astype(jnp.float32) * (2.0 * math.pi / length)
    return (jnp.cos(turns), jnp.sin(turns))

def signed_freq(values, length):
    return jnp.where(values < length // 2, values, values - length).astype(jnp.float32)

def kinetic_table(positions, length):
    rowsq = signed_freq(positions // length, length)
    colsq = signed_freq(positions % length, length)
    depth = signed_freq(jnp.arange(length, dtype=jnp.int32), length)
    total = depth[:, None] ** 2 + (rowsq * rowsq + colsq * colsq)[None, :]
    return total * (8.0 / (length * length))

def inverse_grid(real_part, imag_part, wreal, wimag):
    first_r = jnp.einsum('xk,bpky->bpxy', wreal, real_part, precision=HIGHEST) - jnp.einsum('xk,bpky->bpxy', wimag, imag_part, precision=HIGHEST)
    first_i = jnp.einsum('xk,bpky->bpxy', wreal, imag_part, precision=HIGHEST) + jnp.einsum('xk,bpky->bpxy', wimag, real_part, precision=HIGHEST)
    out_r = jnp.einsum('bpxk,yk->bpxy', first_r, wreal, precision=HIGHEST) - jnp.einsum('bpxk,yk->bpxy', first_i, wimag, precision=HIGHEST)
    out_i = jnp.einsum('bpxk,yk->bpxy', first_r, wimag, precision=HIGHEST) + jnp.einsum('bpxk,yk->bpxy', first_i, wreal, precision=HIGHEST)
    return (out_r, out_i)

def forward_grid(real_part, imag_part, wreal, wimag):
    first_r = jnp.einsum('xk,bpxy->bpky', wreal, real_part, precision=HIGHEST) + jnp.einsum('xk,bpxy->bpky', wimag, imag_part, precision=HIGHEST)
    first_i = jnp.einsum('xk,bpxy->bpky', wreal, imag_part, precision=HIGHEST) - jnp.einsum('xk,bpxy->bpky', wimag, real_part, precision=HIGHEST)
    out_r = jnp.einsum('bpky,yq->bpkq', first_r, wreal, precision=HIGHEST) + jnp.einsum('bpky,yq->bpkq', first_i, wimag, precision=HIGHEST)
    out_i = jnp.einsum('bpky,yq->bpkq', first_i, wreal, precision=HIGHEST) - jnp.einsum('bpky,yq->bpkq', first_r, wimag, precision=HIGHEST)
    return (out_r, out_i)

def to_planes(coeffs, zcos, zsin, length):
    scale = 1.0 / math.sqrt(length)
    real_part = jnp.einsum('pz,bzs->bps', zcos, coeffs[0], precision=HIGHEST) - jnp.einsum('pz,bzs->bps', zsin, coeffs[1], precision=HIGHEST)
    imag_part = jnp.einsum('pz,bzs->bps', zsin, coeffs[0], precision=HIGHEST) + jnp.einsum('pz,bzs->bps', zcos, coeffs[1], precision=HIGHEST)
    return (real_part * scale, imag_part * scale)

def from_planes(real_part, imag_part, zcos, zsin, planes):
    scale = 1.0 / math.sqrt(planes)
    out_r = jnp.einsum('pz,bps->bzs', zcos, real_part, precision=HIGHEST) + jnp.einsum('pz,bps->bzs', zsin, imag_part, precision=HIGHEST)
    out_i = jnp.einsum('pz,bps->bzs', zcos, imag_part, precision=HIGHEST) - jnp.einsum('pz,bps->bzs', zsin, real_part, precision=HIGHEST)
    return jnp.stack([out_r * scale, out_i * scale])

def reference(orbitals, response, potential, perturbation, energies, stick_pos):
    zcos, zsin = phase_tables(SL, GRID, GRID)
    gcos, gsin = phase_tables(GRID, GRID, GRID)
    wreal = gcos / math.sqrt(GRID)
    wimag = gsin / math.sqrt(GRID)
    kinetic = kinetic_table(stick_pos, GRID)

    def place(values):
        empty = jnp.zeros(values.shape[:-1] + (GRID * GRID,), jnp.float32)
        return empty.at[..., stick_pos].set(values).reshape(values.shape[:-1] + (GRID, GRID))

    def one_band(total, items):
        orbital, change, energy = items
        orb_r, orb_i = to_planes(orbital[:, None], zcos, zsin, GRID)
        chg_r, chg_i = to_planes(change[:, None], zcos, zsin, GRID)
        field_r, field_i = inverse_grid(place(orb_r), place(orb_i), wreal, wimag)
        resp_r, resp_i = inverse_grid(place(chg_r), place(chg_i), wreal, wimag)
        total = total + lax.optimization_barrier(jnp.sum(2.0 * (field_r * resp_r + field_i * resp_i), axis=0))
        mixed_r = potential * resp_r + perturbation * field_r
        mixed_i = potential * resp_i + perturbation * field_i
        back_r, back_i = forward_grid(mixed_r, mixed_i, wreal, wimag)
        back_r = back_r.reshape(back_r.shape[:2] + (GRID * GRID,))[..., stick_pos]
        back_i = back_i.reshape(back_i.shape[:2] + (GRID * GRID,))[..., stick_pos]
        applied = from_planes(back_r, back_i, zcos, zsin, SL)[:, 0]
        result = (kinetic - energy) * change + applied
        return (total, result)
    start = jnp.zeros((SL, GRID, GRID), jnp.float32)
    density, stacked = lax.scan(one_band, start, (jnp.moveaxis(orbitals, 1, 0), jnp.moveaxis(response, 1, 0), energies))
    return (jnp.moveaxis(stacked, 0, 1), density)
```

```python
import functools
import math

import numpy as np
import jax
import jax.numpy as jnp
from jax import lax
from jax.experimental import pallas as pl
from jax.experimental.pallas import tpu as pltpu
from jax.sharding import PartitionSpec as P
import ml_dtypes

HIGHEST = lax.Precision.HIGHEST
F32 = jnp.float32
BF16 = jnp.bfloat16
GRID = 360
PAD = 384
ROWS = 45
CHUNK = 48
SLOTS = 8
LANES = 128
VMEM_LIMIT = 60 * 1024 * 1024


def trig(rows, cols):
    turns = (np.outer(rows, cols) % GRID) * (2.0 * math.pi / GRID)
    return np.cos(turns), np.sin(turns)


def split_table(table):
    high = table.astype(np.float32).astype(ml_dtypes.bfloat16)
    low = (table - high.astype(np.float64)).astype(ml_dtypes.bfloat16)
    return high, low


def grid_tables(bands):
    points = np.arange(GRID)
    cos, sin = trig(points, points)
    cos, sin = cos / math.sqrt(GRID), sin / math.sqrt(GRID)
    rows, chunk = GRID // bands, PAD // bands
    spread = (points // rows) * chunk + points % rows

    def block(sign, row_at, col_at):
        full = np.zeros((2 * PAD, 2 * PAD))
        full[np.ix_(row_at, col_at)] = cos
        full[np.ix_(row_at + PAD, col_at + PAD)] = cos
        full[np.ix_(row_at, col_at + PAD)] = sign * sin
        full[np.ix_(row_at + PAD, col_at)] = -sign * sin
        return split_table(full)

    right = block(1.0, points, points)
    left = block(-1.0, spread, points)
    right_back = block(-1.0, points, points)
    left_back = block(1.0, points, spread)
    return right, left, right_back, left_back


def planes_kernel(table_ref, orb_ref, chg_ref, pos_ref, out_ref):
    planes = table_ref.shape[0] // 2
    depth = table_ref.shape[1]
    both = jnp.concatenate(
        [orb_ref[...].reshape(depth, LANES), chg_ref[...].reshape(depth, LANES)], axis=1
    )
    values = jnp.dot(table_ref[...], both, precision=HIGHEST, preferred_element_type=F32)
    pos = pos_ref[...].astype(F32)
    row = jnp.floor((pos + 0.5) * (1.0 / GRID))
    col = pos - row * GRID
    pieces = [
        values[:planes, :LANES],
        values[planes:, :LANES],
        values[:planes, LANES:],
        values[planes:, LANES:],
        jnp.broadcast_to(row, (planes, LANES)),
        jnp.broadcast_to(col, (planes, LANES)),
        jnp.zeros((planes, LANES), F32),
        jnp.zeros((planes, LANES), F32),
    ]
    for slot, piece in enumerate(pieces):
        out_ref[pl.ds(slot, planes, stride=SLOTS), :] = piece


def one_hot_into(out_ref, rows_ref, slot, sources):
    grid_index = lax.broadcasted_iota(jnp.int32, (PAD, LANES), 0).astype(F32)
    for src in range(sources):
        wanted = rows_ref[src * SLOTS + slot : src * SLOTS + slot + 1, :]
        hot = jnp.where(grid_index == wanted, 1.0, 0.0).astype(BF16)
        out_ref[:, src * LANES : (src + 1) * LANES] = hot


def dot3(a_high, a_low, b_high, b_low):
    out = jnp.dot(a_high, b_high, preferred_element_type=F32)
    out += jnp.dot(a_low, b_high, preferred_element_type=F32)
    out += jnp.dot(a_high, b_low, preferred_element_type=F32)
    return out


def halves(x):
    high = x.astype(BF16)
    return high, (x - high.astype(F32)).astype(BF16)


def forward_kernel(
    bands, sources, vals_ref, pot_ref, per_ref, rh_ref, rl_ref, lh_ref, ll_ref, *rest
):
    dens_refs = rest[:bands]
    h_ref = rest[bands]
    row_hot, col_hot, scaled, field, turned, dens, pot, per = rest[bands + 1 :]
    me = lax.axis_index("band")
    one_hot_into(row_hot, vals_ref, 4, sources)
    one_hot_into(col_hot, vals_ref, 5, sources)
    rows, chunk = GRID // bands, PAD // bands
    pot[...] = jnp.zeros_like(pot)
    per[...] = jnp.zeros_like(per)
    for k in range(bands):
        pot[k * chunk : k * chunk + rows, :GRID] = pot_ref[0, k * rows : (k + 1) * rows, :]
        per[k * chunk : k * chunk + rows, :GRID] = per_ref[0, k * rows : (k + 1) * rows, :]

    for comp in range(4):
        for src in range(sources):
            lanes = slice(src * LANES, (src + 1) * LANES)
            value = vals_ref[src * SLOTS + comp : src * SLOTS + comp + 1, :]
            high, low = halves(value)
            hot = col_hot[:, lanes]
            scaled[:PAD, lanes] = hot * high
            scaled[PAD:, lanes] = hot * low
        placed = lax.dot_general(
            row_hot[...], scaled[...], (((1,), (1,)), ((), ())), preferred_element_type=F32
        )
        top, side = (comp // 2) * PAD, (comp % 2) * PAD
        field[top : top + PAD, side : side + PAD] = placed[:, :PAD] + placed[:, PAD:]

    high, low = halves(field[...])
    turned[...] = dot3(high, low, rh_ref[...], rl_ref[...])
    field[:PAD, :PAD] = turned[:PAD, :PAD]
    field[PAD:, :PAD] = turned[:PAD, PAD:]
    field[:PAD, PAD:] = turned[PAD:, :PAD]
    field[PAD:, PAD:] = turned[PAD:, PAD:]
    high, low = halves(field[...])
    turned[...] = dot3(lh_ref[...], ll_ref[...], high, low)
    orb_r, chg_r = turned[:PAD, :PAD], turned[:PAD, PAD:]
    orb_i, chg_i = turned[PAD:, :PAD], turned[PAD:, PAD:]
    dens[...] = (2.0 * (orb_r * chg_r + orb_i * chg_i)).reshape(bands, chunk, PAD)
    h_ref[:, :PAD] = pot[...] * chg_r + per[...] * orb_r
    h_ref[:, PAD:] = pot[...] * chg_i + per[...] * orb_i
    for k in range(bands):
        dens_refs[k][...] = dens[jnp.bitwise_xor(me, k)]


def backward_kernel(
    sources, vals_ref, h_ref, rh_ref, rl_ref, lh_ref, ll_ref, out_ref, col_hot, turned, stacked
):
    grid_index = lax.broadcasted_iota(jnp.int32, (PAD, LANES), 0).astype(F32)
    for src in range(sources):
        wanted = vals_ref[src * SLOTS + 5 : src * SLOTS + 6, :]
        hot = jnp.where(grid_index == wanted, 1.0, 0.0).astype(BF16)
        col_hot[:PAD, src * LANES : (src + 1) * LANES] = hot
        col_hot[PAD:, src * LANES : (src + 1) * LANES] = hot
    high, low = halves(h_ref[...])
    first = dot3(high, low, rh_ref[...], rl_ref[...])
    turned[:PAD, :] = first[:, :PAD]
    turned[PAD:, :] = first[:, PAD:]
    high, low = halves(turned[...])
    grid = dot3(lh_ref[...], ll_ref[...], high, low)
    high, low = halves(grid)
    stacked[:, :PAD] = high
    stacked[:, PAD:] = low
    group = 8

    def some(step, _):
        start = pl.multiple_of(step * (group * LANES), group * LANES)
        chosen = jnp.dot(
            stacked[...], col_hot[:, pl.ds(start, group * LANES)], preferred_element_type=F32
        )
        for k in range(group):
            base = pl.multiple_of((step * group + k) * SLOTS, SLOTS)
            wanted = vals_ref[pl.ds(base, SLOTS), :][4:5, :]
            mask = grid_index == wanted
            lanes = slice(k * LANES, (k + 1) * LANES)
            real = jnp.sum(jnp.where(mask, chosen[:PAD, lanes], 0.0), axis=0, keepdims=True)
            imag = jnp.sum(jnp.where(mask, chosen[PAD:, lanes], 0.0), axis=0, keepdims=True)
            out_ref[pl.ds(base, SLOTS), :] = jnp.concatenate(
                [real, imag, jnp.zeros((SLOTS - 2, LANES), F32)], axis=0
            )
        return 0

    lax.fori_loop(0, sources // group, some, 0)


def residual_kernel(bands, table_ref, back_ref, chg_ref, pos_ref, energy_ref, *rest):
    parts = rest[:bands]
    out_ref, dens_ref = rest[bands:]
    planes = back_ref.shape[0] // SLOTS
    real = back_ref[pl.ds(0, planes, stride=SLOTS), :]
    imag = back_ref[pl.ds(1, planes, stride=SLOTS), :]
    both = jnp.concatenate([real, imag], axis=0)
    applied = jnp.dot(table_ref[...], both, precision=HIGHEST, preferred_element_type=F32)
    pos = pos_ref[...].astype(F32)
    row = jnp.floor((pos + 0.5) * (1.0 / GRID))
    col = pos - row * GRID
    half = GRID // 2
    row = jnp.where(row < half, row, row - GRID)
    col = jnp.where(col < half, col, col - GRID)
    depth = lax.broadcasted_iota(jnp.int32, (GRID, LANES), 0).astype(F32)
    depth = jnp.where(depth < half, depth, depth - GRID)
    kinetic = (depth * depth + (row * row + col * col)) * (8.0 / (GRID * GRID))
    factor = kinetic - energy_ref[0]
    out_ref[0, 0] = factor * chg_ref[0, 0] + applied[:GRID]
    out_ref[1, 0] = factor * chg_ref[1, 0] + applied[GRID:]
    total = parts[0][...]
    for part in parts[1:]:
        total = total + part[...]
    dens_ref[0] = total[: dens_ref.shape[1], :GRID]


def in_vmem(count):
    return [pl.BlockSpec(memory_space=pltpu.VMEM)] * count


def params():
    return pltpu.CompilerParams(vmem_limit_bytes=VMEM_LIMIT)


def on_device(orbitals, response, potential, perturbation, energies, stick_pos):
    planes = lax.axis_size("pw")
    bands = lax.axis_size("band")
    rows, chunk = GRID // bands, PAD // bands
    cos, sin = trig(np.arange(planes), np.arange(GRID))
    to_planes = np.block([[cos, -sin], [sin, cos]]) / math.sqrt(GRID)
    from_planes = np.block([[cos.T, sin.T], [-sin.T, cos.T]]) / math.sqrt(planes)
    right, left, right_back, left_back = grid_tables(bands)
    pos = stick_pos.reshape(1, LANES)

    packed = pl.pallas_call(
        planes_kernel,
        out_shape=jax.ShapeDtypeStruct((planes * SLOTS, LANES), F32),
        in_specs=in_vmem(4),
        out_specs=in_vmem(1)[0],
        compiler_params=params(),
        name="to_planes",
    )(to_planes.astype(np.float32), orbitals, response, pos)
    arrived = lax.all_to_all(
        packed.reshape(planes, SLOTS, LANES), "pw", split_axis=0, concat_axis=0, tiled=True
    ).reshape(planes * SLOTS, LANES)

    total = planes * LANES
    outs = pl.pallas_call(
        functools.partial(forward_kernel, bands, planes),
        out_shape=[jax.ShapeDtypeStruct((chunk, PAD), F32)] * bands
        + [jax.ShapeDtypeStruct((PAD, 2 * PAD), F32)],
        in_specs=in_vmem(7),
        out_specs=in_vmem(bands + 1),
        scratch_shapes=[
            pltpu.VMEM((PAD, total), BF16),
            pltpu.VMEM((PAD, total), BF16),
            pltpu.VMEM((2 * PAD, total), BF16),
            pltpu.VMEM((2 * PAD, 2 * PAD), F32),
            pltpu.VMEM((2 * PAD, 2 * PAD), F32),
            pltpu.VMEM((bands, chunk, PAD), F32),
            pltpu.VMEM((PAD, PAD), F32),
            pltpu.VMEM((PAD, PAD), F32),
        ],
        compiler_params=params(),
        cost_estimate=pl.CostEstimate(
            flops=15_000_000_000, bytes_accessed=8_000_000, transcendentals=0
        ),
        name="place_and_transform",
    )(arrived, potential, perturbation, *right, *left)
    blocks, h = outs[:bands], outs[bands]
    parts = [blocks[0]] + [
        lax.ppermute(blocks[k], "band", [(i, i ^ k) for i in range(bands)])
        for k in range(1, bands)
    ]

    picked = pl.pallas_call(
        functools.partial(backward_kernel, planes),
        out_shape=jax.ShapeDtypeStruct((planes * SLOTS, LANES), F32),
        in_specs=in_vmem(6),
        out_specs=in_vmem(1)[0],
        scratch_shapes=[
            pltpu.VMEM((2 * PAD, total), BF16),
            pltpu.VMEM((2 * PAD, PAD), F32),
            pltpu.VMEM((2 * PAD, 2 * PAD), BF16),
        ],
        compiler_params=params(),
        cost_estimate=pl.CostEstimate(
            flops=8_000_000_000, bytes_accessed=8_000_000, transcendentals=0
        ),
        name="back_and_pick",
    )(arrived, h, *right_back, *left_back)
    returned = lax.all_to_all(
        picked.reshape(planes, SLOTS, LANES), "pw", split_axis=0, concat_axis=0, tiled=True
    ).reshape(planes * SLOTS, LANES)

    specs = in_vmem(4) + [pl.BlockSpec(memory_space=pltpu.SMEM)] + in_vmem(bands)
    residual, density = pl.pallas_call(
        functools.partial(residual_kernel, bands),
        out_shape=[
            jax.ShapeDtypeStruct((2, 1, GRID, LANES), F32),
            jax.ShapeDtypeStruct((1, rows, GRID), F32),
        ],
        in_specs=specs,
        out_specs=in_vmem(2),
        compiler_params=params(),
        name="from_planes",
    )(from_planes.astype(np.float32), returned, response, pos, energies, *parts)
    return (residual, density)


def solution(mesh):
    placed = (
        P(None, "band", None, "pw"),
        P(None, "band", None, "pw"),
        P("pw", None, None),
        P("pw", None, None),
        P("band"),
        P("pw"),
    )
    return jax.shard_map(
        on_device,
        mesh=mesh,
        in_specs=placed,
        out_specs=(P(None, "band", None, "pw"), P("pw", "band", None)),
        check_vma=False,
    )
```

```python
import functools
import math

import numpy as np
import jax
import jax.numpy as jnp
from jax import lax
from jax.experimental import pallas as pl
from jax.experimental.pallas import tpu as pltpu
from jax.sharding import PartitionSpec as P
import ml_dtypes

HIGHEST = lax.Precision.HIGHEST
F32 = jnp.float32
BF16 = jnp.bfloat16
GRID = 360
THIRD = 120
PAD = 384
SLOTS = 8
LANES = 128
WINDOW = 128
TALL = PAD + WINDOW
GROUP = 8
CHUNKS = LANES // GROUP
WIDE = 256
HALF_ROOT3 = math.sqrt(3.0) / 2.0
VMEM_LIMIT = 56 * 1024 * 1024


def trig(rows, cols):
    turns = (np.outer(rows, cols) % GRID) * (2.0 * math.pi / GRID)
    return np.cos(turns), np.sin(turns)


def split_table(table):
    high = table.astype(np.float32).astype(ml_dtypes.bfloat16)
    low = (table - high.astype(np.float64)).astype(ml_dtypes.bfloat16)
    return high, low


def transform_tables():
    small = np.arange(THIRD)
    spread = (small // 15) * 16 + small % 15

    def stack(sign, row_at, col_at, after_is_row):
        full = np.zeros((3 * 2 * LANES, 2 * LANES))
        for turn in range(3):
            after = 3 * small + turn
            if after_is_row:
                cos, sin = trig(after, small)
            else:
                cos, sin = trig(small, after)
            cos, sin = cos / math.sqrt(GRID), sin / math.sqrt(GRID)
            part = np.zeros((2 * LANES, 2 * LANES))
            part[np.ix_(row_at, col_at)] = cos
            part[np.ix_(row_at + LANES, col_at + LANES)] = cos
            part[np.ix_(row_at, col_at + LANES)] = sign * sin
            part[np.ix_(row_at + LANES, col_at)] = -sign * sin
            full[turn * 2 * LANES : (turn + 1) * 2 * LANES] = part
        return split_table(full)

    right = stack(1.0, small, small, False)
    left = stack(-1.0, spread, small, True)
    left_back = stack(1.0, small, spread, False)
    right_back = stack(-1.0, small, small, True)
    return right, left, left_back, right_back


def column_order():
    table = np.zeros((PAD, PAD), np.float32)
    points = np.arange(GRID)
    table[points, (points % 3) * LANES + points // 3] = 1.0
    return table.astype(ml_dtypes.bfloat16)


def halves(x):
    high = x.astype(BF16)
    return high, (x - high.astype(F32)).astype(BF16)


def dot(a, b):
    return jnp.dot(a, b, preferred_element_type=F32)


def dot3(a_high, a_low, b_high, b_low):
    return dot(a_high, b_high) + dot(a_low, b_high) + dot(a_high, b_low)


def three_point(a, b, c, sign):
    sums = [b[k] + c[k] for k in range(2)]
    mids = [a[k] - 0.5 * sums[k] for k in range(2)]
    diffs = [(sign * HALF_ROOT3) * (b[k] - c[k]) for k in range(2)]
    first = (a[0] + sums[0], a[1] + sums[1])
    second = (mids[0] - diffs[1], mids[1] + diffs[0])
    third = (mids[0] + diffs[1], mids[1] - diffs[0])
    return first, second, third


def sort_table(pos):
    across = jnp.broadcast_to(pos, (LANES, LANES))
    rank = jnp.sum(jnp.where(across.T < across, 1.0, 0.0), axis=0, keepdims=True)
    place = lax.broadcasted_iota(jnp.int32, (LANES, LANES), 0).astype(F32)
    return jnp.where(place == rank, 1.0, 0.0)


def exact_dot_t(values, table):
    return lax.dot_general(
        values, table, (((1,), (1,)), ((), ())), precision=HIGHEST, preferred_element_type=F32
    )


def planes_kernel(table_ref, orb_ref, chg_ref, pos_ref, out_ref):
    planes = table_ref.shape[0] // 2
    depth = table_ref.shape[1]
    both = jnp.concatenate(
        [orb_ref[...].reshape(depth, LANES), chg_ref[...].reshape(depth, LANES)], axis=1
    )
    pos = pos_ref[...].astype(F32)
    order = sort_table(pos)
    pos = exact_dot_t(jnp.broadcast_to(pos, (SLOTS, LANES)), order)[0:1, :]
    values = jnp.dot(table_ref[...], both, precision=HIGHEST, preferred_element_type=F32)
    values = exact_dot_t(
        jnp.concatenate([values[:, :LANES], values[:, LANES:]], axis=0), order
    )
    row = jnp.floor((pos + 0.5) * (1.0 / GRID))
    col = pos - row * GRID
    row = row + 8.0 * (jnp.where(row >= THIRD, 1.0, 0.0) + jnp.where(row >= 2 * THIRD, 1.0, 0.0))
    col = col + 8.0 * (jnp.where(col >= THIRD, 1.0, 0.0) + jnp.where(col >= 2 * THIRD, 1.0, 0.0))
    pieces = [values[k * planes : (k + 1) * planes] for k in range(4)] + [
        jnp.broadcast_to(row, (planes, LANES)),
        jnp.broadcast_to(col, (planes, LANES)),
        jnp.zeros((planes, LANES), F32),
        jnp.zeros((planes, LANES), F32),
    ]
    for slot, piece in enumerate(pieces):
        out_ref[pl.ds(slot, planes, stride=SLOTS), :] = piece


def reorder_kernel(pot_ref, per_ref, order_ref, out_ref, lines, rows):
    rows[...] = jnp.zeros_like(rows)
    lines[2 * GRID :, :] = jnp.zeros((GRID, LANES), F32)
    for field, ref in enumerate((pot_ref, per_ref)):
        for j in range(3):
            width = min(LANES, GRID - j * LANES)
            lines[j * GRID : (j + 1) * GRID, :width] = ref[0, :, j * LANES : j * LANES + width]
        for turn in range(3):
            for k in range(8):
                base = turn * LANES + 16 * k
                for j in range(3):
                    start = j * GRID + 45 * k + turn
                    rows[base : base + 15, j * LANES : (j + 1) * LANES] = lines[
                        pl.ds(start, 15, stride=3), :
                    ]
        high, low = halves(rows[...])
        out_ref[field] = dot(high, order_ref[...]) + dot(low, order_ref[...])


def exchange_lanes(blocks):
    group = lax.broadcasted_iota(jnp.int32, (SLOTS, LANES), 1) // GROUP
    blocks = list(blocks)
    for bit in range(4):
        step = 1 << bit
        high = (group & step) != 0
        for i in range(CHUNKS):
            if i & step:
                continue
            a, b = blocks[i], blocks[i + step]
            blocks[i] = jnp.where(high, pltpu.roll(b, GROUP * step, 1), a)
            blocks[i + step] = jnp.where(high, b, pltpu.roll(a, LANES - GROUP * step, 1))
    return blocks


def window_rows(vals, start):
    rows = lax.broadcasted_iota(jnp.int32, (WINDOW, WIDE), 0) + start
    return rows.astype(F32) == vals[4:5, :]


def column_hot(vals):
    cols = lax.broadcasted_iota(jnp.int32, (PAD, WIDE), 0).astype(F32)
    return jnp.where(cols == vals[5:6, :], 1.0, 0.0).astype(BF16)


def forward_kernel(
    vals_ref, pot_ref, rh_ref, rl_ref, lh_ref, ll_ref,
    keep_ref, send_ref, hh_ref, hl_ref, group_ref, win_ref,
    field, xh, xl, zh, zl, dens,
):
    core = lax.axis_index("band") % 2
    field[...] = jnp.zeros_like(field)
    for half in range(2):
        blocks = [
            vals_ref[(half * CHUNKS + j) * SLOTS : (half * CHUNKS + j + 1) * SLOTS, :]
            for j in range(CHUNKS)
        ]
        for q, block in enumerate(exchange_lanes(blocks)):
            group_ref[q * SLOTS : (q + 1) * SLOTS, half * LANES : (half + 1) * LANES] = block
    most = 0
    for q in range(CHUNKS):
        rows = group_ref[q * SLOTS + 4 : q * SLOTS + 5, :]
        low = jnp.min(rows).astype(jnp.int32)
        high = jnp.max(rows).astype(jnp.int32)
        start = jnp.bitwise_and(low, -16)
        count = lax.shift_right_logical(high - start, 7) + 1
        win_ref[q] = start
        win_ref[CHUNKS + q] = count
        most = jnp.maximum(most, count)
    win_ref[2 * CHUNKS] = most

    def place(q, start):
        vals = group_ref[pl.ds(pl.multiple_of(q * SLOTS, SLOTS), SLOTS), :]
        hot = jnp.where(window_rows(vals, start), 1.0, 0.0).astype(BF16)
        cols = column_hot(vals)
        scaled = []
        for comp in range(4):
            high, low = halves(vals[comp : comp + 1, :])
            scaled.append(jnp.concatenate([hot * high, hot * low], axis=1))
        placed = lax.dot_general(
            jnp.concatenate(scaled, axis=0),
            jnp.concatenate([cols, cols], axis=1),
            (((1,), (1,)), ((), ())),
            preferred_element_type=F32,
        )
        for comp in range(4):
            field[comp, pl.ds(start, WINDOW), :] += placed[comp * WINDOW : (comp + 1) * WINDOW]

    @pl.when(most == 1)
    def _():
        def four(step, _):
            for k in range(4):
                place(4 * step + k, pl.multiple_of(win_ref[4 * step + k], 16))
            return 0

        lax.fori_loop(0, CHUNKS // 4, four, 0)

    @pl.when(most > 1)
    def _():
        def one(q, _):
            def block(b, _):
                place(q, pl.multiple_of(win_ref[q] + b * WINDOW, 16))
                return 0

            lax.fori_loop(0, win_ref[CHUNKS + q], block, 0)
            return 0

        lax.fori_loop(0, CHUNKS, one, 0)

    step = 16
    for f in range(2):
        for r in range(0, LANES, step):
            rows = []
            for r2 in range(3):
                at = slice(r2 * LANES + r, r2 * LANES + r + step)
                cols = [
                    tuple(field[2 * f + k, at, c2 * LANES : (c2 + 1) * LANES] for k in range(2))
                    for c2 in range(3)
                ]
                rows.append(three_point(*cols, 1.0))
            for y2 in range(3):
                turned = three_point(rows[0][y2], rows[1][y2], rows[2][y2], 1.0)
                for x2 in range(3):
                    for k in range(2):
                        at = slice(f * PAD + x2 * LANES + r, f * PAD + x2 * LANES + r + step)
                        lanes = slice(y2 * WIDE + k * LANES, y2 * WIDE + (k + 1) * LANES)
                        high, low = halves(turned[x2][k])
                        xh[at, lanes] = high
                        xl[at, lanes] = low

    for y2 in range(3):
        at = slice(y2 * WIDE, (y2 + 1) * WIDE)
        out = dot3(xh[:, at], xl[:, at], rh_ref[at, :], rl_ref[at, :])
        for f in range(2):
            for x2 in range(3):
                for k in range(2):
                    part = out[
                        f * PAD + x2 * LANES : f * PAD + (x2 + 1) * LANES,
                        k * LANES : (k + 1) * LANES,
                    ]
                    rows = slice(x2 * WIDE + k * LANES, x2 * WIDE + (k + 1) * LANES)
                    lanes = slice(f * PAD + y2 * LANES, f * PAD + (y2 + 1) * LANES)
                    high, low = halves(part)
                    zh[rows, lanes] = high
                    zl[rows, lanes] = low

    for x2 in range(3):
        at = slice(x2 * WIDE, (x2 + 1) * WIDE)
        out = dot3(lh_ref[at, :], ll_ref[at, :], zh[at, :], zl[at, :])
        orb_r, chg_r = out[:LANES, :PAD], out[:LANES, PAD:]
        orb_i, chg_i = out[LANES:, :PAD], out[LANES:, PAD:]
        dens[x2] = 2.0 * (orb_r * chg_r + orb_i * chg_i)
        pot = pot_ref[0, x2 * LANES : (x2 + 1) * LANES, :]
        per = pot_ref[1, x2 * LANES : (x2 + 1) * LANES, :]
        for k, (chg, orb) in enumerate(((chg_r, orb_r), (chg_i, orb_i))):
            high, low = halves(pot * chg + per * orb)
            rows = slice(x2 * WIDE + k * LANES, x2 * WIDE + (k + 1) * LANES)
            hh_ref[rows, :] = high
            hl_ref[rows, :] = low
    for m in range(4):
        for x2 in range(3):
            own = pl.multiple_of(16 * (2 * m + core), 16)
            other = pl.multiple_of(16 * (2 * m + 1 - core), 16)
            keep_ref[m, 16 * x2 : 16 * (x2 + 1), :] = dens[x2, pl.ds(own, 16), :]
            send_ref[m, 16 * x2 : 16 * (x2 + 1), :] = dens[x2, pl.ds(other, 16), :]


def back_kernel(hh_ref, hl_ref, lh_ref, ll_ref, rh_ref, rl_ref, out_ref, mid, ph, plow):
    for x2 in range(3):
        at = slice(x2 * WIDE, (x2 + 1) * WIDE)
        mid[at, :] = dot3(lh_ref[at, :], ll_ref[at, :], hh_ref[at, :], hl_ref[at, :])
    step = 16
    for r in range(0, LANES, step):
        for y2 in range(3):
            lanes = slice(y2 * LANES, (y2 + 1) * LANES)
            parts = [
                tuple(
                    mid[x2 * WIDE + k * LANES + r : x2 * WIDE + k * LANES + r + step, lanes]
                    for k in range(2)
                )
                for x2 in range(3)
            ]
            for r2, pair in enumerate(three_point(*parts, -1.0)):
                for k in range(2):
                    high, low = halves(pair[k])
                    rows = slice(r2 * LANES + r, r2 * LANES + r + step)
                    to = slice(y2 * WIDE + k * LANES, y2 * WIDE + (k + 1) * LANES)
                    ph[rows, to] = high
                    plow[rows, to] = low
    for y2 in range(3):
        at = slice(y2 * WIDE, (y2 + 1) * WIDE)
        out = dot3(ph[:, at], plow[:, at], rh_ref[at, :], rl_ref[at, :])
        mid[:PAD, y2 * LANES : (y2 + 1) * LANES] = out[:, :LANES]
        mid[PAD:, y2 * LANES : (y2 + 1) * LANES] = out[:, LANES:]
    for r in range(0, PAD, step):
        parts = [
            tuple(
                mid[k * PAD + r : k * PAD + r + step, y2 * LANES : (y2 + 1) * LANES]
                for k in range(2)
            )
            for y2 in range(3)
        ]
        for q2, pair in enumerate(three_point(*parts, -1.0)):
            for k in range(2):
                high, low = halves(pair[k])
                out_ref[k, r : r + step, q2 * LANES : (q2 + 1) * LANES] = high
                out_ref[k, r : r + step, PAD + q2 * LANES : PAD + (q2 + 1) * LANES] = low
    out_ref[:, PAD:, :] = jnp.zeros((2, WINDOW, 2 * PAD), BF16)


def pick_kernel(grid_ref, group_ref, win_ref, keep_ref, got_ref, out_ref, *rest):
    block_refs, (picked, total) = rest[:4], rest[4:]
    chip = lax.axis_index("band") // 2
    total[...] = keep_ref[...] + got_ref[...]
    for k in range(4):
        block_refs[k][...] = total[jnp.bitwise_xor(chip, k)]

    def pick(q, start):
        vals = group_ref[pl.ds(pl.multiple_of(q * SLOTS, SLOTS), SLOTS), :]
        mask = window_rows(vals, start)
        cols = column_hot(vals)
        lines = grid_ref[:, pl.ds(start, WINDOW), :].reshape(2 * WINDOW, 2 * PAD)
        chosen = dot(lines, jnp.concatenate([cols, cols], axis=0))
        real = jnp.sum(jnp.where(mask, chosen[:WINDOW], 0.0), axis=0, keepdims=True)
        imag = jnp.sum(jnp.where(mask, chosen[WINDOW:], 0.0), axis=0, keepdims=True)
        return jnp.concatenate([real, imag, jnp.zeros((SLOTS - 2, WIDE), F32)], axis=0)

    most = win_ref[2 * CHUNKS]

    @pl.when(most == 1)
    def _():
        def four(step, _):
            for k in range(4):
                q = 4 * step + k
                at = pl.ds(pl.multiple_of(q * SLOTS, SLOTS), SLOTS)
                picked[at, :] = pick(q, pl.multiple_of(win_ref[q], 16))
            return 0

        lax.fori_loop(0, CHUNKS // 4, four, 0)

    @pl.when(most > 1)
    def _():
        picked[...] = jnp.zeros_like(picked)

        def one(q, _):
            at = pl.ds(pl.multiple_of(q * SLOTS, SLOTS), SLOTS)

            def block(b, _):
                picked[at, :] += pick(q, pl.multiple_of(win_ref[q] + b * WINDOW, 16))
                return 0

            lax.fori_loop(0, win_ref[CHUNKS + q], block, 0)
            return 0

        lax.fori_loop(0, CHUNKS, one, 0)

    for half in range(2):
        blocks = [
            picked[q * SLOTS : (q + 1) * SLOTS, half * LANES : (half + 1) * LANES]
            for q in range(CHUNKS)
        ]
        for j, block in enumerate(exchange_lanes(blocks)):
            src = half * CHUNKS + j
            out_ref[src * SLOTS : (src + 1) * SLOTS, :] = block


def residual_kernel(table_ref, order_ref, back_ref, chg_ref, pos_ref, energy_ref, *rest):
    parts = rest[:4]
    out_ref, dens_ref = rest[4:]
    planes = back_ref.shape[0] // SLOTS
    pos = pos_ref[...].astype(F32)
    order = sort_table(pos)
    real = back_ref[pl.ds(0, planes, stride=SLOTS), :]
    imag = back_ref[pl.ds(1, planes, stride=SLOTS), :]
    both = jnp.concatenate([real, imag], axis=0)
    both = jnp.dot(both, order, precision=HIGHEST, preferred_element_type=F32)
    applied = jnp.dot(table_ref[...], both, precision=HIGHEST, preferred_element_type=F32)
    row = jnp.floor((pos + 0.5) * (1.0 / GRID))
    col = pos - row * GRID
    half = GRID // 2
    row = jnp.where(row < half, row, row - GRID)
    col = jnp.where(col < half, col, col - GRID)
    depth = lax.broadcasted_iota(jnp.int32, (GRID, LANES), 0).astype(F32)
    depth = jnp.where(depth < half, depth, depth - GRID)
    kinetic = (depth * depth + (row * row + col * col)) * (8.0 / (GRID * GRID))
    factor = kinetic - energy_ref[0]
    out_ref[0, 0] = factor * chg_ref[0, 0] + applied[:GRID]
    out_ref[1, 0] = factor * chg_ref[1, 0] + applied[GRID:]
    high, low = halves(parts[0][...] + parts[1][...] + parts[2][...] + parts[3][...])
    turned = (((1,), (1,)), ((), ()))
    total = lax.dot_general(high, order_ref[...], turned, preferred_element_type=F32)
    total += lax.dot_general(low, order_ref[...], turned, preferred_element_type=F32)
    for i in range(15):
        for x2 in range(3):
            dens_ref[3 * i + x2] = total[16 * x2 + i : 16 * x2 + i + 1, :GRID]


def in_vmem(count):
    return [pl.BlockSpec(memory_space=pltpu.VMEM)] * count


def in_smem():
    return pl.BlockSpec(memory_space=pltpu.SMEM)


def call(kernel, name, outs, ins, out_specs, scratch=(), flops=0):
    return pl.pallas_call(
        kernel,
        out_shape=outs,
        in_specs=ins,
        out_specs=out_specs,
        scratch_shapes=list(scratch),
        compiler_params=pltpu.CompilerParams(vmem_limit_bytes=VMEM_LIMIT),
        cost_estimate=pl.CostEstimate(flops=flops, bytes_accessed=3_000_000, transcendentals=0),
        name=name,
    )


def shape(*dims, dtype=F32):
    return jax.ShapeDtypeStruct(dims, dtype)


def on_device(orbitals, response, potential, perturbation, energies, stick_pos):
    planes = lax.axis_size("pw")
    bands = lax.axis_size("band")
    cos, sin = trig(np.arange(planes), np.arange(GRID))
    to_planes = np.block([[cos, -sin], [sin, cos]]) / math.sqrt(GRID)
    from_planes = np.block([[cos.T, sin.T], [-sin.T, cos.T]]) / math.sqrt(planes)
    right, left, left_back, right_back = transform_tables()
    order = column_order()
    pos = stick_pos.reshape(1, LANES)

    packed = call(
        planes_kernel, "to_planes", shape(planes * SLOTS, LANES), in_vmem(4), in_vmem(1)[0],
        flops=500_000_000,
    )(to_planes.astype(np.float32), orbitals, response, pos)
    arrived = lax.all_to_all(
        packed.reshape(planes, SLOTS, LANES), "pw", split_axis=0, concat_axis=0, tiled=True
    ).reshape(planes * SLOTS, LANES)
    pots = call(
        reorder_kernel, "reorder", shape(2, PAD, PAD), in_vmem(3), in_vmem(1)[0],
        [pltpu.VMEM((3 * GRID, LANES), F32), pltpu.VMEM((PAD, PAD), F32)],
        flops=1_500_000_000,
    )(potential, perturbation, order)

    keep, send, h_high, h_low, group, windows = call(
        forward_kernel,
        "place_and_transform",
        [
            shape(4, 48, PAD),
            shape(4, 48, PAD),
            shape(2 * PAD, PAD, dtype=BF16),
            shape(2 * PAD, PAD, dtype=BF16),
            shape(CHUNKS * SLOTS, WIDE),
            shape(2 * CHUNKS + 1, dtype=jnp.int32),
        ],
        in_vmem(6),
        in_vmem(5) + [in_smem()],
        [
            pltpu.VMEM((4, TALL, PAD), F32),
            pltpu.VMEM((2 * PAD, 2 * PAD), BF16),
            pltpu.VMEM((2 * PAD, 2 * PAD), BF16),
            pltpu.VMEM((2 * PAD, 2 * PAD), BF16),
            pltpu.VMEM((2 * PAD, 2 * PAD), BF16),
            pltpu.VMEM((3, LANES, PAD), F32),
        ],
        flops=10_000_000_000,
    )(arrived, pots, *right, *left)
    got = lax.ppermute(send, "band", [(i, i ^ 1) for i in range(bands)])
    grid = call(
        back_kernel,
        "back",
        shape(2, TALL, 2 * PAD, dtype=BF16),
        in_vmem(6),
        in_vmem(1)[0],
        [
            pltpu.VMEM((2 * PAD, PAD), F32),
            pltpu.VMEM((PAD, 2 * PAD), BF16),
            pltpu.VMEM((PAD, 2 * PAD), BF16),
        ],
        flops=3_000_000_000,
    )(h_high, h_low, *left_back, *right_back)
    picked, *blocks = call(
        pick_kernel,
        "pick",
        [shape(planes * SLOTS, LANES)] + [shape(48, PAD)] * 4,
        in_vmem(2) + [in_smem()] + in_vmem(2),
        in_vmem(5),
        [pltpu.VMEM((CHUNKS * SLOTS, WIDE), F32), pltpu.VMEM((4, 48, PAD), F32)],
        flops=5_000_000_000,
    )(grid, group, windows, keep, got)
    returned = lax.all_to_all(
        picked.reshape(planes, SLOTS, LANES), "pw", split_axis=0, concat_axis=0, tiled=True
    ).reshape(planes * SLOTS, LANES)
    parts = [blocks[0]] + [
        lax.ppermute(blocks[k], "band", [(i, i ^ (2 * k)) for i in range(bands)])
        for k in range(1, 4)
    ]

    residual, density = call(
        residual_kernel,
        "from_planes",
        [shape(2, 1, GRID, LANES), shape(GRID // bands, 1, GRID)],
        in_vmem(5) + [in_smem()] + in_vmem(4),
        in_vmem(2),
        flops=500_000_000,
    )(from_planes.astype(np.float32), order, returned, response, pos, energies, *parts)
    return (residual, density.reshape(1, GRID // bands, GRID))


def solution(mesh):
    placed = (
        P(None, "band", None, "pw"),
        P(None, "band", None, "pw"),
        P("pw", None, None),
        P("pw", None, None),
        P("band"),
        P("pw"),
    )
    return jax.shard_map(
        on_device,
        mesh=mesh,
        in_specs=placed,
        out_specs=(P(None, "band", None, "pw"), P("pw", "band", None)),
        check_vma=False,
    )
```

```python
import functools
import math

import numpy as np
import jax
import jax.numpy as jnp
from jax import lax
from jax.experimental import pallas as pl
from jax.experimental.pallas import tpu as pltpu
from jax.sharding import PartitionSpec as P
import ml_dtypes

F32 = jnp.float32
BF16 = jnp.bfloat16
GRID = 360
THIRD = 120
PAD = 384
SLOTS = 8
LANES = 128
WINDOW = 128
TALL = PAD + WINDOW
GROUP = 8
CHUNKS = LANES // GROUP
WIDE = 256
HALF_ROOT3 = math.sqrt(3.0) / 2.0


def trig(rows, cols):
    turns = (np.outer(rows, cols) % GRID) * (2.0 * math.pi / GRID)
    return np.cos(turns), np.sin(turns)


def split_table(table):
    high = table.astype(np.float32).astype(ml_dtypes.bfloat16)
    low = (table - high.astype(np.float64)).astype(ml_dtypes.bfloat16)
    return high, low


def transform_tables():
    small = np.arange(THIRD)
    spread = (small // 15) * 16 + small % 15

    def stack(sign, row_at, col_at, after_is_row):
        full = np.zeros((3 * 2 * LANES, 2 * LANES))
        for turn in range(3):
            after = 3 * small + turn
            if after_is_row:
                cos, sin = trig(after, small)
            else:
                cos, sin = trig(small, after)
            cos, sin = cos / math.sqrt(GRID), sin / math.sqrt(GRID)
            part = np.zeros((2 * LANES, 2 * LANES))
            part[np.ix_(row_at, col_at)] = cos
            part[np.ix_(row_at + LANES, col_at + LANES)] = cos
            part[np.ix_(row_at, col_at + LANES)] = sign * sin
            part[np.ix_(row_at + LANES, col_at)] = -sign * sin
            full[turn * 2 * LANES : (turn + 1) * 2 * LANES] = part
        return split_table(full)

    right = stack(1.0, small, small, False)
    left = stack(-1.0, spread, small, True)
    left_back = stack(1.0, small, spread, False)
    right_back = stack(-1.0, small, small, True)
    return right, left, left_back, right_back


def column_order():
    table = np.zeros((PAD, PAD), np.float32)
    points = np.arange(GRID)
    table[points, (points % 3) * LANES + points // 3] = 1.0
    return table.astype(ml_dtypes.bfloat16)


def halves(x):
    high = x.astype(BF16)
    return high, (x - high.astype(F32)).astype(BF16)


def dot(a, b):
    return jnp.dot(a, b, preferred_element_type=F32)


def dot3(a_high, a_low, b_high, b_low):
    return dot(a_high, b_high) + dot(a_low, b_high) + dot(a_high, b_low)


def three_point(a, b, c, sign):
    sums = [b[k] + c[k] for k in range(2)]
    mids = [a[k] - 0.5 * sums[k] for k in range(2)]
    diffs = [(sign * HALF_ROOT3) * (b[k] - c[k]) for k in range(2)]
    first = (a[0] + sums[0], a[1] + sums[1])
    second = (mids[0] - diffs[1], mids[1] + diffs[0])
    third = (mids[0] + diffs[1], mids[1] - diffs[0])
    return first, second, third


def sort_table(pos):
    across = jnp.broadcast_to(pos, (LANES, LANES))
    rank = jnp.sum(jnp.where(across.T < across, 1.0, 0.0), axis=0, keepdims=True)
    place = lax.broadcasted_iota(jnp.int32, (LANES, LANES), 0).astype(F32)
    return jnp.where(place == rank, 1.0, 0.0)


def dot_t(a, b):
    return lax.dot_general(a, b, (((1,), (1,)), ((), ())), preferred_element_type=F32)


def copy_in(pairs, sems):
    copies = [pltpu.make_async_copy(src, dst, sems.at[k]) for k, (src, dst) in enumerate(pairs)]
    for copy in copies:
        copy.start()
    return copies


def planes_kernel(pos_any, table_any, orb_any, chg_any, out_ref, pos_ref, table, data, sems):
    planes = out_ref.shape[0] // SLOTS
    copies = copy_in(
        [
            (pos_any, pos_ref),
            (orb_any.at[:, 0], data.at[0:2]),
            (chg_any.at[:, 0], data.at[2:4]),
            (table_any, table),
        ],
        sems,
    )
    copies[0].wait()
    pos = pos_ref[...].astype(F32)
    order = sort_table(pos).astype(BF16)
    row = jnp.floor((pos + 0.5) * (1.0 / GRID))
    col = pos - row * GRID
    row = row + 8.0 * (jnp.where(row >= THIRD, 1.0, 0.0) + jnp.where(row >= 2 * THIRD, 1.0, 0.0))
    col = col + 8.0 * (jnp.where(col >= THIRD, 1.0, 0.0) + jnp.where(col >= 2 * THIRD, 1.0, 0.0))
    place = jnp.concatenate([row, col, jnp.zeros((SLOTS - 2, LANES), F32)], axis=0)
    high, low = halves(place)
    place = dot_t(high, order) + dot_t(low, order)
    for slot in range(4, SLOTS):
        line = place[slot - 4 : slot - 3, :]
        out_ref[pl.ds(slot, planes, stride=SLOTS), :] = jnp.broadcast_to(line, (planes, LANES))
    for copy in copies[1:]:
        copy.wait()
    both = jnp.concatenate(
        [
            data[0:2].reshape(2 * GRID, LANES),
            data[2:4].reshape(2 * GRID, LANES),
        ],
        axis=1,
    )
    high, low = halves(both)
    values = dot3(table[0], table[1], high, low)
    high, low = halves(jnp.concatenate([values[:, :LANES], values[:, LANES:]], axis=0))
    values = dot_t(high, order) + dot_t(low, order)
    for slot in range(4):
        out_ref[pl.ds(slot, planes, stride=SLOTS), :] = values[
            slot * planes : (slot + 1) * planes
        ]


def reorder_kernel(pot_ref, per_ref, order_ref, out_ref, lines, rows):
    rows[...] = jnp.zeros_like(rows)
    lines[2 * GRID :, :] = jnp.zeros((GRID, LANES), F32)
    for field, ref in enumerate((pot_ref, per_ref)):
        for j in range(3):
            width = min(LANES, GRID - j * LANES)
            lines[j * GRID : (j + 1) * GRID, :width] = ref[0, :, j * LANES : j * LANES + width]
        for turn in range(3):
            for k in range(8):
                base = turn * LANES + 16 * k
                for j in range(3):
                    start = j * GRID + 45 * k + turn
                    rows[base : base + 15, j * LANES : (j + 1) * LANES] = lines[
                        pl.ds(start, 15, stride=3), :
                    ]
        high, low = halves(rows[...])
        out_ref[field] = dot(high, order_ref[...]) + dot(low, order_ref[...])


def exchange_lanes(blocks):
    group = lax.broadcasted_iota(jnp.int32, (SLOTS, LANES), 1) // GROUP
    blocks = list(blocks)
    for bit in range(4):
        step = 1 << bit
        high = (group & step) != 0
        for i in range(CHUNKS):
            if i & step:
                continue
            a, b = blocks[i], blocks[i + step]
            blocks[i] = jnp.where(high, pltpu.roll(b, GROUP * step, 1), a)
            blocks[i + step] = jnp.where(high, b, pltpu.roll(a, LANES - GROUP * step, 1))
    return blocks


def window_rows(vals, start):
    rows = lax.broadcasted_iota(jnp.int32, (WINDOW, WIDE), 0) + start
    return rows.astype(F32) == vals[4:5, :]


def column_hot(vals):
    cols = lax.broadcasted_iota(jnp.int32, (PAD, WIDE), 0).astype(F32)
    return jnp.where(cols == vals[5:6, :], 1.0, 0.0).astype(BF16)


def find_windows(group, win):
    most = 0
    for q in range(CHUNKS):
        rows = group[q * SLOTS + 4 : q * SLOTS + 5, :]
        low = jnp.min(rows).astype(jnp.int32)
        high = jnp.max(rows).astype(jnp.int32)
        start = jnp.bitwise_and(low, -16)
        count = lax.shift_right_logical(high - start, 7) + 1
        win[q] = start
        win[CHUNKS + q] = count
        most = jnp.maximum(most, count)
    return most


def over_windows(work, most, win):
    @pl.when(most == 1)
    def _():
        def four(step, _):
            for k in range(4):
                work(4 * step + k, pl.multiple_of(win[4 * step + k], 16))
            return 0

        lax.fori_loop(0, CHUNKS // 4, four, 0)

    @pl.when(most > 1)
    def _():
        def one(q, _):
            def block(b, _):
                work(q, pl.multiple_of(win[q] + b * WINDOW, 16))
                return 0

            lax.fori_loop(0, win[CHUNKS + q], block, 0)
            return 0

        lax.fori_loop(0, CHUNKS, one, 0)


def forward_kernel(
    vals_ref, pot_ref, rh_ref, rl_ref, lh_ref, ll_ref,
    keep_ref, send_ref, hh_ref, hl_ref, group_ref,
    win_ref, field, xh, xl, zh, zl, dens,
):
    core = lax.axis_index("band") % 2
    field[...] = jnp.zeros_like(field)
    for half in range(2):
        blocks = [
            vals_ref[(half * CHUNKS + j) * SLOTS : (half * CHUNKS + j + 1) * SLOTS, :]
            for j in range(CHUNKS)
        ]
        for q, block in enumerate(exchange_lanes(blocks)):
            group_ref[q * SLOTS : (q + 1) * SLOTS, half * LANES : (half + 1) * LANES] = block
    most = find_windows(group_ref, win_ref)

    def place(q, start):
        vals = group_ref[pl.ds(pl.multiple_of(q * SLOTS, SLOTS), SLOTS), :]
        hot = jnp.where(window_rows(vals, start), 1.0, 0.0).astype(BF16)
        cols = column_hot(vals)
        scaled = []
        for comp in range(4):
            high, low = halves(vals[comp : comp + 1, :])
            scaled.append(jnp.concatenate([hot * high, hot * low], axis=1))
        placed = lax.dot_general(
            jnp.concatenate(scaled, axis=0),
            jnp.concatenate([cols, cols], axis=1),
            (((1,), (1,)), ((), ())),
            preferred_element_type=F32,
        )
        for comp in range(4):
            field[comp, pl.ds(start, WINDOW), :] += placed[comp * WINDOW : (comp + 1) * WINDOW]

    over_windows(place, most, win_ref)

    step = 16
    for f in range(2):
        for r in range(0, LANES, step):
            rows = []
            for r2 in range(3):
                at = slice(r2 * LANES + r, r2 * LANES + r + step)
                cols = [
                    tuple(field[2 * f + k, at, c2 * LANES : (c2 + 1) * LANES] for k in range(2))
                    for c2 in range(3)
                ]
                rows.append(three_point(*cols, 1.0))
            for y2 in range(3):
                turned = three_point(rows[0][y2], rows[1][y2], rows[2][y2], 1.0)
                for x2 in range(3):
                    for k in range(2):
                        at = slice(f * PAD + x2 * LANES + r, f * PAD + x2 * LANES + r + step)
                        lanes = slice(y2 * WIDE + k * LANES, y2 * WIDE + (k + 1) * LANES)
                        high, low = halves(turned[x2][k])
                        xh[at, lanes] = high
                        xl[at, lanes] = low

    for y2 in range(3):
        at = slice(y2 * WIDE, (y2 + 1) * WIDE)
        out = dot3(xh[:, at], xl[:, at], rh_ref[at, :], rl_ref[at, :])
        for f in range(2):
            for x2 in range(3):
                for k in range(2):
                    part = out[
                        f * PAD + x2 * LANES : f * PAD + (x2 + 1) * LANES,
                        k * LANES : (k + 1) * LANES,
                    ]
                    rows = slice(x2 * WIDE + k * LANES, x2 * WIDE + (k + 1) * LANES)
                    lanes = slice(f * PAD + y2 * LANES, f * PAD + (y2 + 1) * LANES)
                    high, low = halves(part)
                    zh[rows, lanes] = high
                    zl[rows, lanes] = low

    for x2 in range(3):
        at = slice(x2 * WIDE, (x2 + 1) * WIDE)
        out = dot3(lh_ref[at, :], ll_ref[at, :], zh[at, :], zl[at, :])
        orb_r, chg_r = out[:LANES, :PAD], out[:LANES, PAD:]
        orb_i, chg_i = out[LANES:, :PAD], out[LANES:, PAD:]
        dens[x2] = 2.0 * (orb_r * chg_r + orb_i * chg_i)
        pot = pot_ref[0, x2 * LANES : (x2 + 1) * LANES, :]
        per = pot_ref[1, x2 * LANES : (x2 + 1) * LANES, :]
        for k, (chg, orb) in enumerate(((chg_r, orb_r), (chg_i, orb_i))):
            high, low = halves(pot * chg + per * orb)
            rows = slice(x2 * WIDE + k * LANES, x2 * WIDE + (k + 1) * LANES)
            hh_ref[rows, :] = high
            hl_ref[rows, :] = low
        for m in range(4):
            own = pl.multiple_of(16 * (2 * m + core), 16)
            other = pl.multiple_of(16 * (2 * m + 1 - core), 16)
            keep_ref[m, 16 * x2 : 16 * (x2 + 1), :] = dens[x2, pl.ds(own, 16), :]
            send_ref[m, 16 * x2 : 16 * (x2 + 1), :] = dens[x2, pl.ds(other, 16), :]


def back_kernel(
    group_ref, hh_ref, hl_ref, lh_ref, ll_ref, rh_ref, rl_ref, out_ref,
    mid, ph, plow, grid, picked, win,
):
    grid[:, PAD:, :] = jnp.zeros((2, WINDOW, 2 * PAD), BF16)
    for x2 in range(3):
        at = slice(x2 * WIDE, (x2 + 1) * WIDE)
        mid[at, :] = dot3(lh_ref[at, :], ll_ref[at, :], hh_ref[at, :], hl_ref[at, :])
    step = 16
    for r in range(0, LANES, step):
        for y2 in range(3):
            lanes = slice(y2 * LANES, (y2 + 1) * LANES)
            parts = [
                tuple(
                    mid[x2 * WIDE + k * LANES + r : x2 * WIDE + k * LANES + r + step, lanes]
                    for k in range(2)
                )
                for x2 in range(3)
            ]
            for r2, pair in enumerate(three_point(*parts, -1.0)):
                for k in range(2):
                    high, low = halves(pair[k])
                    rows = slice(r2 * LANES + r, r2 * LANES + r + step)
                    to = slice(y2 * WIDE + k * LANES, y2 * WIDE + (k + 1) * LANES)
                    ph[rows, to] = high
                    plow[rows, to] = low
    most = find_windows(group_ref, win)
    for y2 in range(3):
        at = slice(y2 * WIDE, (y2 + 1) * WIDE)
        out = dot3(ph[:, at], plow[:, at], rh_ref[at, :], rl_ref[at, :])
        mid[:PAD, y2 * LANES : (y2 + 1) * LANES] = out[:, :LANES]
        mid[PAD:, y2 * LANES : (y2 + 1) * LANES] = out[:, LANES:]
    for r in range(0, PAD, step):
        parts = [
            tuple(
                mid[k * PAD + r : k * PAD + r + step, y2 * LANES : (y2 + 1) * LANES]
                for k in range(2)
            )
            for y2 in range(3)
        ]
        for q2, pair in enumerate(three_point(*parts, -1.0)):
            for k in range(2):
                high, low = halves(pair[k])
                grid[k, r : r + step, q2 * LANES : (q2 + 1) * LANES] = high
                grid[k, r : r + step, PAD + q2 * LANES : PAD + (q2 + 1) * LANES] = low
    picked[...] = jnp.zeros_like(picked)

    def pick(q, start):
        at = pl.ds(pl.multiple_of(q * SLOTS, SLOTS), SLOTS)
        vals = group_ref[at, :]
        mask = window_rows(vals, start)
        cols = column_hot(vals)
        lines = grid[:, pl.ds(start, WINDOW), :].reshape(2 * WINDOW, 2 * PAD)
        chosen = dot(lines, jnp.concatenate([cols, cols], axis=0))
        real = jnp.sum(jnp.where(mask, chosen[:WINDOW], 0.0), axis=0, keepdims=True)
        imag = jnp.sum(jnp.where(mask, chosen[WINDOW:], 0.0), axis=0, keepdims=True)
        picked[at, :] += jnp.concatenate(
            [real, imag, jnp.zeros((SLOTS - 2, WIDE), F32)], axis=0
        )

    over_windows(pick, most, win)
    for half in range(2):
        blocks = [
            picked[q * SLOTS : (q + 1) * SLOTS, half * LANES : (half + 1) * LANES]
            for q in range(CHUNKS)
        ]
        for j, block in enumerate(exchange_lanes(blocks)):
            src = half * CHUNKS + j
            out_ref[src * SLOTS : (src + 1) * SLOTS, :] = block


def pair_kernel(keep_ref, got_ref, *rest):
    block_refs, total = rest[:4], rest[4]
    chip = lax.axis_index("band") // 2
    total[...] = keep_ref[...] + got_ref[...]
    for k in range(4):
        block_refs[k][...] = total[jnp.bitwise_xor(chip, k)]


def residual_kernel(
    pos_ref, table, order_ref, chg_ref, back_ref, energy_ref, *rest
):
    parts, (out_ref, dens_ref) = rest[:4], rest[4:]
    planes = back_ref.shape[0] // SLOTS
    pos = pos_ref[...].astype(F32)
    order = sort_table(pos).astype(BF16)
    row = jnp.floor((pos + 0.5) * (1.0 / GRID))
    col = pos - row * GRID
    half = GRID // 2
    row = jnp.where(row < half, row, row - GRID)
    col = jnp.where(col < half, col, col - GRID)
    depth = lax.broadcasted_iota(jnp.int32, (GRID, LANES), 0).astype(F32)
    depth = jnp.where(depth < half, depth, depth - GRID)
    kinetic = (depth * depth + (row * row + col * col)) * (8.0 / (GRID * GRID))
    factor = kinetic - energy_ref[0]
    real = back_ref[pl.ds(0, planes, stride=SLOTS), :]
    imag = back_ref[pl.ds(1, planes, stride=SLOTS), :]
    high, low = halves(jnp.concatenate([real, imag], axis=0))
    both = dot(jnp.concatenate([high, low], axis=0), order).astype(BF16)
    applied = dot(table[...], jnp.concatenate([both, both[: 2 * planes]], axis=0))
    for k in range(2):
        out_ref[k, 0] = factor * chg_ref[k, 0] + applied[k * GRID : (k + 1) * GRID]
    high, low = halves(parts[0][...] + parts[1][...] + parts[2][...] + parts[3][...])
    total = dot_t(high, order_ref[...]) + dot_t(low, order_ref[...])
    for i in range(15):
        for x2 in range(3):
            dens_ref[3 * i + x2] = total[16 * x2 + i : 16 * x2 + i + 1, :GRID]


def in_vmem(count):
    return [pl.BlockSpec(memory_space=pltpu.VMEM)] * count


def in_hbm(count):
    return [pl.BlockSpec(memory_space=pltpu.HBM)] * count


def in_smem():
    return pl.BlockSpec(memory_space=pltpu.SMEM)


def call(kernel, name, outs, ins, out_specs, scratch=(), flops=0, limit=32):
    return pl.pallas_call(
        kernel,
        out_shape=outs,
        in_specs=ins,
        out_specs=out_specs,
        scratch_shapes=list(scratch),
        compiler_params=pltpu.CompilerParams(vmem_limit_bytes=limit * 1024 * 1024),
        cost_estimate=pl.CostEstimate(flops=flops, bytes_accessed=3_000_000, transcendentals=0),
        name=name,
    )


def shape(*dims, dtype=F32):
    return jax.ShapeDtypeStruct(dims, dtype)


def sems(count):
    return pltpu.SemaphoreType.DMA((count,))


def on_device(orbitals, response, potential, perturbation, energies, stick_pos):
    planes = lax.axis_size("pw")
    bands = lax.axis_size("band")
    cos, sin = trig(np.arange(planes), np.arange(GRID))
    to_planes = np.block([[cos, -sin], [sin, cos]]) / math.sqrt(GRID)
    to_planes = np.stack(split_table(to_planes))
    from_planes = np.block([[cos.T, sin.T], [-sin.T, cos.T]]) / math.sqrt(planes)
    high, low = split_table(from_planes)
    from_planes = np.concatenate([high, high, low], axis=1)
    right, left, left_back, right_back = transform_tables()
    order = column_order()
    pos = stick_pos.reshape(1, LANES)
    square = pltpu.VMEM((2 * PAD, 2 * PAD), BF16)
    grouped = pltpu.VMEM((CHUNKS * SLOTS, WIDE), F32)
    windows = pltpu.SMEM((2 * CHUNKS,), jnp.int32)

    packed = call(
        planes_kernel,
        "to_planes",
        shape(planes * SLOTS, LANES),
        in_hbm(4),
        in_vmem(1)[0],
        [
            pltpu.VMEM((1, LANES), jnp.int32),
            pltpu.VMEM(to_planes.shape, BF16),
            pltpu.VMEM((4, GRID, LANES), F32),
            sems(4),
        ],
        flops=500_000_000,
        limit=60,
    )(pos, to_planes, orbitals, response)
    arrived = lax.all_to_all(
        packed.reshape(planes, SLOTS, LANES), "pw", split_axis=0, concat_axis=0, tiled=True
    ).reshape(planes * SLOTS, LANES)
    pots = call(
        reorder_kernel,
        "reorder",
        shape(2, PAD, PAD),
        in_vmem(3),
        in_vmem(1)[0],
        [pltpu.VMEM((3 * GRID, LANES), F32), pltpu.VMEM((PAD, PAD), F32)],
        flops=1_500_000_000,
        limit=60,
    )(potential, perturbation, order)

    keep, send, h_high, h_low, group = call(
        forward_kernel,
        "place_and_transform",
        [
            shape(4, 48, PAD),
            shape(4, 48, PAD),
            shape(2 * PAD, PAD, dtype=BF16),
            shape(2 * PAD, PAD, dtype=BF16),
            shape(CHUNKS * SLOTS, WIDE),
        ],
        in_vmem(6),
        in_vmem(5),
        [windows, pltpu.VMEM((4, TALL, PAD), F32)]
        + [square] * 4
        + [pltpu.VMEM((3, LANES, PAD), F32)],
        flops=10_000_000_000,
    )(arrived, pots, *right, *left)
    got = lax.ppermute(send, "band", [(i, i ^ 1) for i in range(bands)])
    picked = call(
        back_kernel,
        "back_and_pick",
        shape(planes * SLOTS, LANES),
        in_vmem(7),
        in_vmem(1)[0],
        [
            pltpu.VMEM((2 * PAD, PAD), F32),
            pltpu.VMEM((PAD, 2 * PAD), BF16),
            pltpu.VMEM((PAD, 2 * PAD), BF16),
            pltpu.VMEM((2, TALL, 2 * PAD), BF16),
            grouped,
            windows,
        ],
        flops=6_000_000_000,
    )(group, h_high, h_low, *left_back, *right_back)
    returned = lax.all_to_all(
        picked.reshape(planes, SLOTS, LANES), "pw", split_axis=0, concat_axis=0, tiled=True
    ).reshape(planes * SLOTS, LANES)
    blocks = call(
        pair_kernel,
        "pair_sum",
        [shape(48, PAD)] * 4,
        in_vmem(2),
        in_vmem(4),
        [pltpu.VMEM((4, 48, PAD), F32)],
        flops=300_000,
    )(keep, got)
    parts = [blocks[0]] + [
        lax.ppermute(blocks[k], "band", [(i, i ^ (2 * k)) for i in range(bands)])
        for k in range(1, 4)
    ]

    residual, density = call(
        residual_kernel,
        "from_planes",
        [shape(2, 1, GRID, LANES), shape(GRID // bands, 1, GRID)],
        in_vmem(5) + [in_smem()] + in_vmem(4),
        in_vmem(2),
        flops=500_000_000,
    )(pos, from_planes, order, response, returned, energies, *parts)
    return (residual, density.reshape(1, GRID // bands, GRID))


def solution(mesh):
    placed = (
        P(None, "band", None, "pw"),
        P(None, "band", None, "pw"),
        P("pw", None, None),
        P("pw", None, None),
        P("band"),
        P("pw"),
    )
    return jax.shard_map(
        on_device,
        mesh=mesh,
        in_specs=placed,
        out_specs=(P(None, "band", None, "pw"), P("pw", "band", None)),
        check_vma=False,
    )
```

```python
import functools
import math

import numpy as np
import jax
import jax.numpy as jnp
from jax import lax
from jax.experimental import pallas as pl
from jax.experimental.pallas import tpu as pltpu
from jax.sharding import PartitionSpec as P
import ml_dtypes

F32 = jnp.float32
BF16 = jnp.bfloat16
GRID = 360
THIRD = 120
PAD = 384
SLOTS = 8
LANES = 128
WINDOW = 128
FIRST = (64, 96, 112) + (128,) * 10 + (112, 96, 80)
TALL = PAD + WINDOW
GROUP = 8
CHUNKS = LANES // GROUP
WIDE = 256
HALF_ROOT3 = math.sqrt(3.0) / 2.0


def trig(rows, cols):
    turns = (np.outer(rows, cols) % GRID) * (2.0 * math.pi / GRID)
    return np.cos(turns), np.sin(turns)


def split_table(table):
    high = table.astype(np.float32).astype(ml_dtypes.bfloat16)
    low = (table - high.astype(np.float64)).astype(ml_dtypes.bfloat16)
    return high, low


def transform_tables():
    small = np.arange(THIRD)
    spread = (small // 15) * 16 + small % 15

    def stack(sign, row_at, col_at, after_is_row):
        full = np.zeros((3 * 2 * LANES, 2 * LANES))
        for turn in range(3):
            after = 3 * small + turn
            if after_is_row:
                cos, sin = trig(after, small)
            else:
                cos, sin = trig(small, after)
            cos, sin = cos / math.sqrt(GRID), sin / math.sqrt(GRID)
            part = np.zeros((2 * LANES, 2 * LANES))
            part[np.ix_(row_at, col_at)] = cos
            part[np.ix_(row_at + LANES, col_at + LANES)] = cos
            part[np.ix_(row_at, col_at + LANES)] = sign * sin
            part[np.ix_(row_at + LANES, col_at)] = -sign * sin
            full[turn * 2 * LANES : (turn + 1) * 2 * LANES] = part
        return split_table(full)

    right = stack(1.0, small, small, False)
    left = stack(-1.0, spread, small, True)
    left_back = stack(1.0, small, spread, False)
    right_back = stack(-1.0, small, small, True)
    return right, left, left_back, right_back


def column_order():
    table = np.zeros((PAD, PAD), np.float32)
    points = np.arange(GRID)
    table[points, (points % 3) * LANES + points // 3] = 1.0
    return table.astype(ml_dtypes.bfloat16)


def halves(x):
    high = x.astype(BF16)
    return high, (x - high.astype(F32)).astype(BF16)


def dot(a, b):
    return jnp.dot(a, b, preferred_element_type=F32)


def dot3(a_high, a_low, b_high, b_low):
    return dot(a_high, b_high) + dot(a_low, b_high) + dot(a_high, b_low)


def three_point(a, b, c, sign):
    sums = [b[k] + c[k] for k in range(2)]
    mids = [a[k] - 0.5 * sums[k] for k in range(2)]
    diffs = [(sign * HALF_ROOT3) * (b[k] - c[k]) for k in range(2)]
    first = (a[0] + sums[0], a[1] + sums[1])
    second = (mids[0] - diffs[1], mids[1] + diffs[0])
    third = (mids[0] + diffs[1], mids[1] - diffs[0])
    return first, second, third


def sort_table(pos):
    across = jnp.broadcast_to(pos, (LANES, LANES))
    rank = jnp.sum(jnp.where(across.T < across, 1.0, 0.0), axis=0, keepdims=True)
    place = lax.broadcasted_iota(jnp.int32, (LANES, LANES), 0).astype(F32)
    return jnp.where(place == rank, 1.0, 0.0)


def dot_t(a, b):
    return lax.dot_general(a, b, (((1,), (1,)), ((), ())), preferred_element_type=F32)


def copy_in(pairs, sems):
    copies = [pltpu.make_async_copy(src, dst, sems.at[k]) for k, (src, dst) in enumerate(pairs)]
    for copy in copies:
        copy.start()
    return copies


def planes_kernel(pos_any, table_any, orb_any, chg_any, out_ref, pos_ref, table, data, sems):
    planes = out_ref.shape[0] // SLOTS
    copies = copy_in(
        [
            (pos_any, pos_ref),
            (orb_any.at[:, 0], data.at[0:2]),
            (chg_any.at[:, 0], data.at[2:4]),
            (table_any, table),
        ],
        sems,
    )
    copies[0].wait()
    pos = pos_ref[...].astype(F32)
    order = sort_table(pos).astype(BF16)
    row = jnp.floor((pos + 0.5) * (1.0 / GRID))
    col = pos - row * GRID
    row = row + 8.0 * (jnp.where(row >= THIRD, 1.0, 0.0) + jnp.where(row >= 2 * THIRD, 1.0, 0.0))
    col = col + 8.0 * (jnp.where(col >= THIRD, 1.0, 0.0) + jnp.where(col >= 2 * THIRD, 1.0, 0.0))
    place = jnp.concatenate([row, col, jnp.zeros((SLOTS - 2, LANES), F32)], axis=0)
    high, low = halves(place)
    place = dot_t(high, order) + dot_t(low, order)
    for slot in range(4, SLOTS):
        line = place[slot - 4 : slot - 3, :]
        out_ref[pl.ds(slot, planes, stride=SLOTS), :] = jnp.broadcast_to(line, (planes, LANES))
    for copy in copies[1:]:
        copy.wait()
    both = jnp.concatenate(
        [
            data[0:2].reshape(2 * GRID, LANES),
            data[2:4].reshape(2 * GRID, LANES),
        ],
        axis=1,
    )
    high, low = halves(both)
    values = dot3(table[0], table[1], high, low)
    high, low = halves(jnp.concatenate([values[:, :LANES], values[:, LANES:]], axis=0))
    values = dot_t(high, order) + dot_t(low, order)
    for slot in range(4):
        out_ref[pl.ds(slot, planes, stride=SLOTS), :] = values[
            slot * planes : (slot + 1) * planes
        ]


def reorder_kernel(pot_ref, per_ref, order_ref, out_ref, done_ref, lines, rows):
    done_ref[0] = 0
    rows[...] = jnp.zeros_like(rows)
    lines[2 * GRID :, :] = jnp.zeros((GRID, LANES), F32)
    for field, ref in enumerate((pot_ref, per_ref)):
        for j in range(3):
            width = min(LANES, GRID - j * LANES)
            lines[j * GRID : (j + 1) * GRID, :width] = ref[0, :, j * LANES : j * LANES + width]
        for turn in range(3):
            for k in range(8):
                base = turn * LANES + 16 * k
                for j in range(3):
                    start = j * GRID + 45 * k + turn
                    rows[base : base + 15, j * LANES : (j + 1) * LANES] = lines[
                        pl.ds(start, 15, stride=3), :
                    ]
        high, low = halves(rows[...])
        out_ref[field] = dot(high, order_ref[...]) + dot(low, order_ref[...])


def exchange_lanes(blocks):
    group = lax.broadcasted_iota(jnp.int32, (SLOTS, LANES), 1) // GROUP
    blocks = list(blocks)
    for bit in range(4):
        step = 1 << bit
        high = (group & step) != 0
        for i in range(CHUNKS):
            if i & step:
                continue
            a, b = blocks[i], blocks[i + step]
            blocks[i] = jnp.where(high, pltpu.roll(b, GROUP * step, 1), a)
            blocks[i + step] = jnp.where(high, b, pltpu.roll(a, LANES - GROUP * step, 1))
    return blocks


def window_rows(vals, start, count):
    rows = lax.broadcasted_iota(jnp.int32, (count, WIDE), 0) + start
    return rows.astype(F32) == vals[4:5, :]


def column_hot(vals):
    cols = lax.broadcasted_iota(jnp.int32, (PAD, WIDE), 0).astype(F32)
    return jnp.where(cols == vals[5:6, :], 1.0, 0.0).astype(BF16)


def find_windows(group, win):
    most = 0
    for q in range(CHUNKS):
        rows = group[q * SLOTS + 4 : q * SLOTS + 5, :]
        low = jnp.min(rows).astype(jnp.int32)
        high = jnp.max(rows).astype(jnp.int32)
        start = jnp.bitwise_and(low, -16)
        more = lax.shift_right_logical(high - start + (WINDOW - FIRST[q]), 7)
        win[q] = start
        win[CHUNKS + q] = start + FIRST[q]
        win[2 * CHUNKS + q] = more
        most = jnp.maximum(most, more)
    return most


def over_windows(work, most, win):
    for q in range(CHUNKS):
        work(q, pl.multiple_of(win[q], 16), FIRST[q], True)

    @pl.when(most > 0)
    def _():
        def one(q, _):
            def block(b, _):
                work(q, pl.multiple_of(win[CHUNKS + q] + b * WINDOW, 16), WINDOW, False)
                return 0

            lax.fori_loop(0, win[2 * CHUNKS + q], block, 0)
            return 0

        lax.fori_loop(0, CHUNKS, one, 0)


def forward_kernel(
    done_ref, vals_ref, rh_ref, rl_ref, lh_ref, ll_ref,
    keep_ref, send_ref, real_ref, group_ref,
    win_ref, field, xh, xl, zh, zl, dens,
):
    core = lax.axis_index("band") % 2
    field[...] = jnp.zeros_like(field)
    for half in range(2):
        blocks = [
            vals_ref[(half * CHUNKS + j) * SLOTS : (half * CHUNKS + j + 1) * SLOTS, :]
            for j in range(CHUNKS)
        ]
        for q, block in enumerate(exchange_lanes(blocks)):
            group_ref[q * SLOTS : (q + 1) * SLOTS, half * LANES : (half + 1) * LANES] = block
    most = find_windows(group_ref, win_ref)

    def place(q, start, count, first):
        vals = group_ref[pl.ds(q * SLOTS if first else pl.multiple_of(q * SLOTS, SLOTS), SLOTS), :]
        hot = jnp.where(window_rows(vals, start, count), 1.0, 0.0).astype(BF16)
        cols = column_hot(vals)
        scaled = []
        for comp in range(4):
            high, low = halves(vals[comp : comp + 1, :])
            scaled.append(jnp.concatenate([hot * high, hot * low], axis=1))
        placed = lax.dot_general(
            jnp.concatenate(scaled, axis=0),
            jnp.concatenate([cols, cols], axis=1),
            (((1,), (1,)), ((), ())),
            preferred_element_type=F32,
        )
        for comp in range(4):
            field[comp, pl.ds(start, count), :] += placed[comp * count : (comp + 1) * count]

    over_windows(place, most, win_ref)

    step = 16
    for f in range(2):
        for r in range(0, LANES, step):
            rows = []
            for r2 in range(3):
                at = slice(r2 * LANES + r, r2 * LANES + r + step)
                cols = [
                    tuple(field[2 * f + k, at, c2 * LANES : (c2 + 1) * LANES] for k in range(2))
                    for c2 in range(3)
                ]
                rows.append(three_point(*cols, 1.0))
            for y2 in range(3):
                turned = three_point(rows[0][y2], rows[1][y2], rows[2][y2], 1.0)
                for x2 in range(3):
                    for k in range(2):
                        at = slice(f * PAD + x2 * LANES + r, f * PAD + x2 * LANES + r + step)
                        lanes = slice(y2 * WIDE + k * LANES, y2 * WIDE + (k + 1) * LANES)
                        high, low = halves(turned[x2][k])
                        xh[at, lanes] = high
                        xl[at, lanes] = low

    for y2 in range(3):
        at = slice(y2 * WIDE, (y2 + 1) * WIDE)
        out = dot3(xh[:, at], xl[:, at], rh_ref[at, :], rl_ref[at, :])
        for f in range(2):
            for x2 in range(3):
                for k in range(2):
                    part = out[
                        f * PAD + x2 * LANES : f * PAD + (x2 + 1) * LANES,
                        k * LANES : (k + 1) * LANES,
                    ]
                    rows = slice(x2 * WIDE + k * LANES, x2 * WIDE + (k + 1) * LANES)
                    lanes = slice(f * PAD + y2 * LANES, f * PAD + (y2 + 1) * LANES)
                    high, low = halves(part)
                    zh[rows, lanes] = high
                    zl[rows, lanes] = low

    for x2 in range(3):
        at = slice(x2 * WIDE, (x2 + 1) * WIDE)
        out = dot3(lh_ref[at, :], ll_ref[at, :], zh[at, :], zl[at, :])
        real_ref[at, :] = out
        dens[x2] = 2.0 * (out[:LANES, :PAD] * out[:LANES, PAD:] + out[LANES:, :PAD] * out[LANES:, PAD:])
        for m in range(4):
            own = pl.multiple_of(16 * (2 * m + core), 16)
            other = pl.multiple_of(16 * (2 * m + 1 - core), 16)
            keep_ref[m, 16 * x2 : 16 * (x2 + 1), :] = dens[x2, pl.ds(own, 16), :]
            send_ref[m, 16 * x2 : 16 * (x2 + 1), :] = dens[x2, pl.ds(other, 16), :]


def back_kernel(
    group_ref, real_ref, pot_ref, lh_ref, ll_ref, rh_ref, rl_ref, out_ref, done_ref,
    mid, ph, plow, grid, picked, win,
):
    done_ref[0] = 0
    grid[:, PAD:, :] = jnp.zeros((2, WINDOW, 2 * PAD), BF16)
    for x2 in range(3):
        at = slice(x2 * WIDE, (x2 + 1) * WIDE)
        rows = slice(x2 * LANES, (x2 + 1) * LANES)
        pot = jnp.concatenate([pot_ref[0, rows, :]] * 2, axis=0)
        per = jnp.concatenate([pot_ref[1, rows, :]] * 2, axis=0)
        high, low = halves(pot * real_ref[at, PAD:] + per * real_ref[at, :PAD])
        mid[at, :] = dot3(lh_ref[at, :], ll_ref[at, :], high, low)
    step = 16
    for r in range(0, LANES, step):
        for y2 in range(3):
            lanes = slice(y2 * LANES, (y2 + 1) * LANES)
            parts = [
                tuple(
                    mid[x2 * WIDE + k * LANES + r : x2 * WIDE + k * LANES + r + step, lanes]
                    for k in range(2)
                )
                for x2 in range(3)
            ]
            for r2, pair in enumerate(three_point(*parts, -1.0)):
                for k in range(2):
                    high, low = halves(pair[k])
                    rows = slice(r2 * LANES + r, r2 * LANES + r + step)
                    to = slice(y2 * WIDE + k * LANES, y2 * WIDE + (k + 1) * LANES)
                    ph[rows, to] = high
                    plow[rows, to] = low
    most = find_windows(group_ref, win)
    for y2 in range(3):
        at = slice(y2 * WIDE, (y2 + 1) * WIDE)
        out = dot3(ph[:, at], plow[:, at], rh_ref[at, :], rl_ref[at, :])
        mid[:PAD, y2 * LANES : (y2 + 1) * LANES] = out[:, :LANES]
        mid[PAD:, y2 * LANES : (y2 + 1) * LANES] = out[:, LANES:]
    for r in range(0, PAD, step):
        parts = [
            tuple(
                mid[k * PAD + r : k * PAD + r + step, y2 * LANES : (y2 + 1) * LANES]
                for k in range(2)
            )
            for y2 in range(3)
        ]
        for q2, pair in enumerate(three_point(*parts, -1.0)):
            for k in range(2):
                high, low = halves(pair[k])
                grid[k, r : r + step, q2 * LANES : (q2 + 1) * LANES] = high
                grid[k, r : r + step, PAD + q2 * LANES : PAD + (q2 + 1) * LANES] = low

    def pick(q, start, count, first):
        at = pl.ds(q * SLOTS if first else pl.multiple_of(q * SLOTS, SLOTS), SLOTS)
        vals = group_ref[at, :]
        mask = window_rows(vals, start, count)
        cols = column_hot(vals)
        lines = grid[:, pl.ds(start, count), :].reshape(2 * count, 2 * PAD)
        chosen = dot(lines, jnp.concatenate([cols, cols], axis=0))
        real = jnp.sum(jnp.where(mask, chosen[:count], 0.0), axis=0, keepdims=True)
        imag = jnp.sum(jnp.where(mask, chosen[count:], 0.0), axis=0, keepdims=True)
        found = jnp.concatenate([real, imag, jnp.zeros((SLOTS - 2, WIDE), F32)], axis=0)
        picked[at, :] = found if first else picked[at, :] + found

    over_windows(pick, most, win)
    for half in range(2):
        blocks = [
            picked[q * SLOTS : (q + 1) * SLOTS, half * LANES : (half + 1) * LANES]
            for q in range(CHUNKS)
        ]
        for j, block in enumerate(exchange_lanes(blocks)):
            src = half * CHUNKS + j
            out_ref[2 * src : 2 * src + 2, :] = block[0:2, :]


def pair_kernel(done_ref, keep_ref, got_ref, *rest):
    block_refs, total = rest[:4], rest[4]
    chip = lax.axis_index("band") // 2
    total[...] = keep_ref[...] + got_ref[...]
    for k in range(4):
        block_refs[k][...] = total[jnp.bitwise_xor(chip, k)]


def residual_kernel(
    pos_ref, table, order_ref, chg_ref, back_ref, energy_ref, *rest
):
    parts, (out_ref, dens_ref) = rest[:4], rest[4:]
    lines = back_ref.shape[0]
    pos = pos_ref[...].astype(F32)
    order = sort_table(pos).astype(BF16)
    row = jnp.floor((pos + 0.5) * (1.0 / GRID))
    col = pos - row * GRID
    half = GRID // 2
    row = jnp.where(row < half, row, row - GRID)
    col = jnp.where(col < half, col, col - GRID)
    depth = lax.broadcasted_iota(jnp.int32, (GRID, LANES), 0).astype(F32)
    depth = jnp.where(depth < half, depth, depth - GRID)
    kinetic = (depth * depth + (row * row + col * col)) * (8.0 / (GRID * GRID))
    factor = kinetic - energy_ref[0]
    high, low = halves(back_ref[...])
    both = dot(jnp.concatenate([high, low], axis=0), order).astype(BF16)
    applied = dot(table[...], jnp.concatenate([both, both[:lines]], axis=0))
    for k in range(2):
        out_ref[k, 0] = factor * chg_ref[k, 0] + applied[k * GRID : (k + 1) * GRID]
    high, low = halves(parts[0][...] + parts[1][...] + parts[2][...] + parts[3][...])
    total = dot_t(high, order_ref[...]) + dot_t(low, order_ref[...])
    for i in range(15):
        for x2 in range(3):
            dens_ref[3 * i + x2] = total[16 * x2 + i : 16 * x2 + i + 1, :GRID]


def in_vmem(count):
    return [pl.BlockSpec(memory_space=pltpu.VMEM)] * count


def in_hbm(count):
    return [pl.BlockSpec(memory_space=pltpu.HBM)] * count


def in_smem():
    return pl.BlockSpec(memory_space=pltpu.SMEM)


def call(kernel, name, outs, ins, out_specs, scratch=(), flops=0, limit=32):
    return pl.pallas_call(
        kernel,
        out_shape=outs,
        in_specs=ins,
        out_specs=out_specs,
        scratch_shapes=list(scratch),
        compiler_params=pltpu.CompilerParams(vmem_limit_bytes=limit * 1024 * 1024),
        cost_estimate=pl.CostEstimate(flops=flops, bytes_accessed=3_000_000, transcendentals=0),
        name=name,
    )


def shape(*dims, dtype=F32):
    return jax.ShapeDtypeStruct(dims, dtype)


def sems(count):
    return pltpu.SemaphoreType.DMA((count,))


def on_device(orbitals, response, potential, perturbation, energies, stick_pos):
    planes = lax.axis_size("pw")
    bands = lax.axis_size("band")
    cos, sin = trig(np.arange(planes), np.arange(GRID))
    to_planes = np.block([[cos, -sin], [sin, cos]]) / math.sqrt(GRID)
    to_planes = np.stack(split_table(to_planes))
    from_planes = np.block([[cos.T, sin.T], [-sin.T, cos.T]]) / math.sqrt(planes)
    from_planes = from_planes.reshape(2 * GRID, 2, planes).swapaxes(1, 2).reshape(2 * GRID, -1)
    high, low = split_table(from_planes)
    from_planes = np.concatenate([high, high, low], axis=1)
    right, left, left_back, right_back = transform_tables()
    order = column_order()
    pos = stick_pos.reshape(1, LANES)
    square = pltpu.VMEM((2 * PAD, 2 * PAD), BF16)
    grouped = pltpu.VMEM((CHUNKS * SLOTS, WIDE), F32)
    windows = pltpu.SMEM((3 * CHUNKS,), jnp.int32)

    packed = call(
        planes_kernel,
        "to_planes",
        shape(planes * SLOTS, LANES),
        in_hbm(4),
        in_vmem(1)[0],
        [
            pltpu.VMEM((1, LANES), jnp.int32),
            pltpu.VMEM(to_planes.shape, BF16),
            pltpu.VMEM((4, GRID, LANES), F32),
            sems(4),
        ],
        flops=500_000_000,
        limit=60,
    )(pos, to_planes, orbitals, response)
    arrived = lax.all_to_all(
        packed.reshape(planes, SLOTS, LANES), "pw", split_axis=0, concat_axis=0, tiled=True
    ).reshape(planes * SLOTS, LANES)
    pots, done = call(
        reorder_kernel,
        "reorder",
        [shape(2, PAD, PAD), shape(1, dtype=jnp.int32)],
        in_vmem(3),
        in_vmem(1) + [in_smem()],
        [pltpu.VMEM((3 * GRID, LANES), F32), pltpu.VMEM((PAD, PAD), F32)],
        flops=1_500_000_000,
        limit=60,
    )(potential, perturbation, order)

    keep, send, fields, group = call(
        forward_kernel,
        "place_and_transform",
        [
            shape(4, 48, PAD),
            shape(4, 48, PAD),
            shape(2 * PAD, 2 * PAD),
            shape(CHUNKS * SLOTS, WIDE),
        ],
        [in_smem()] + in_vmem(5),
        in_vmem(4),
        [windows, pltpu.VMEM((4, TALL, PAD), F32)]
        + [square] * 4
        + [pltpu.VMEM((3, LANES, PAD), F32)],
        flops=10_000_000_000,
    )(done, arrived, *right, *left)
    got = lax.ppermute(send, "band", [(i, i ^ 1) for i in range(bands)])
    picked, done = call(
        back_kernel,
        "back_and_pick",
        [shape(2 * planes, LANES), shape(1, dtype=jnp.int32)],
        in_vmem(7),
        in_vmem(1) + [in_smem()],
        [
            pltpu.VMEM((2 * PAD, PAD), F32),
            pltpu.VMEM((PAD, 2 * PAD), BF16),
            pltpu.VMEM((PAD, 2 * PAD), BF16),
            pltpu.VMEM((2, TALL, 2 * PAD), BF16),
            grouped,
            windows,
        ],
        flops=6_000_000_000,
    )(group, fields, pots, *left_back, *right_back)
    returned = lax.all_to_all(picked, "pw", split_axis=0, concat_axis=0, tiled=True)
    blocks = call(
        pair_kernel,
        "pair_sum",
        [shape(48, PAD)] * 4,
        [in_smem()] + in_vmem(2),
        in_vmem(4),
        [pltpu.VMEM((4, 48, PAD), F32)],
        flops=300_000,
    )(done, keep, got)
    parts = [blocks[0]] + [
        lax.ppermute(blocks[k], "band", [(i, i ^ (2 * k)) for i in range(bands)])
        for k in range(1, 4)
    ]

    residual, density = call(
        residual_kernel,
        "from_planes",
        [shape(2, 1, GRID, LANES), shape(GRID // bands, 1, GRID)],
        in_vmem(5) + [in_smem()] + in_vmem(4),
        in_vmem(2),
        flops=500_000_000,
    )(pos, from_planes, order, response, returned, energies, *parts)
    return (residual, density.reshape(1, GRID // bands, GRID))


def solution(mesh):
    placed = (
        P(None, "band", None, "pw"),
        P(None, "band", None, "pw"),
        P("pw", None, None),
        P("pw", None, None),
        P("band"),
        P("pw"),
    )
    return jax.shard_map(
        on_device,
        mesh=mesh,
        in_specs=placed,
        out_specs=(P(None, "band", None, "pw"), P("pw", "band", None)),
        check_vma=False,
    )
```

```python
import functools
import math

import numpy as np
import jax
import jax.numpy as jnp
from jax import lax
from jax.experimental import pallas as pl
from jax.experimental.pallas import tpu as pltpu
from jax.sharding import PartitionSpec as P
import ml_dtypes

F32 = jnp.float32
BF16 = jnp.bfloat16
GRID = 360
THIRD = 120
PAD = 384
SLOTS = 8
LANES = 128
WINDOW = 128
FIRST = (64, 96, 112) + (128,) * 10 + (112, 96, 80)
TALL = PAD + WINDOW
GROUP = 8
CHUNKS = LANES // GROUP
WIDE = 256
HALF_ROOT3 = math.sqrt(3.0) / 2.0


def trig(rows, cols):
    turns = (np.outer(rows, cols) % GRID) * (2.0 * math.pi / GRID)
    return np.cos(turns), np.sin(turns)


def split_table(table):
    high = table.astype(np.float32).astype(ml_dtypes.bfloat16)
    low = (table - high.astype(np.float64)).astype(ml_dtypes.bfloat16)
    return high, low


def transform_tables():
    small = np.arange(THIRD)
    spread = (small // 15) * 16 + small % 15

    def stack(sign, row_at, col_at, after_is_row):
        full = np.zeros((3 * 2 * LANES, 2 * LANES))
        for turn in range(3):
            after = 3 * small + turn
            if after_is_row:
                cos, sin = trig(after, small)
            else:
                cos, sin = trig(small, after)
            cos, sin = cos / math.sqrt(GRID), sin / math.sqrt(GRID)
            part = np.zeros((2 * LANES, 2 * LANES))
            part[np.ix_(row_at, col_at)] = cos
            part[np.ix_(row_at + LANES, col_at + LANES)] = cos
            part[np.ix_(row_at, col_at + LANES)] = sign * sin
            part[np.ix_(row_at + LANES, col_at)] = -sign * sin
            full[turn * 2 * LANES : (turn + 1) * 2 * LANES] = part
        return split_table(full)

    right = stack(1.0, small, small, False)
    left = stack(-1.0, spread, small, True)
    left_back = stack(1.0, small, spread, False)
    right_back = stack(-1.0, small, small, True)
    return right, left, left_back, right_back


def column_order():
    table = np.zeros((PAD, PAD), np.float32)
    points = np.arange(GRID)
    table[points, (points % 3) * LANES + points // 3] = 1.0
    return table.astype(ml_dtypes.bfloat16)


def halves(x):
    high = x.astype(BF16)
    return high, (x - high.astype(F32)).astype(BF16)


def dot(a, b):
    return jnp.dot(a, b, preferred_element_type=F32)


def dot3(a_high, a_low, b_high, b_low):
    return dot(a_high, b_high) + dot(a_low, b_high) + dot(a_high, b_low)


def three_point(a, b, c, sign):
    sums = [b[k] + c[k] for k in range(2)]
    mids = [a[k] - 0.5 * sums[k] for k in range(2)]
    diffs = [(sign * HALF_ROOT3) * (b[k] - c[k]) for k in range(2)]
    first = (a[0] + sums[0], a[1] + sums[1])
    second = (mids[0] - diffs[1], mids[1] + diffs[0])
    third = (mids[0] + diffs[1], mids[1] - diffs[0])
    return first, second, third


def sort_table(pos):
    across = jnp.broadcast_to(pos, (LANES, LANES))
    rank = jnp.sum(jnp.where(across.T < across, 1.0, 0.0), axis=0, keepdims=True)
    place = lax.broadcasted_iota(jnp.int32, (LANES, LANES), 0).astype(F32)
    return jnp.where(place == rank, 1.0, 0.0)


def dot_t(a, b):
    return lax.dot_general(a, b, (((1,), (1,)), ((), ())), preferred_element_type=F32)


def copy_in(pairs, sems):
    copies = [pltpu.make_async_copy(src, dst, sems.at[k]) for k, (src, dst) in enumerate(pairs)]
    for copy in copies:
        copy.start()
    return copies


def planes_kernel(pos_any, table_any, orb_any, chg_any, out_ref, pos_ref, table, data, sems):
    planes = out_ref.shape[0] // SLOTS
    copies = copy_in(
        [
            (pos_any, pos_ref),
            (orb_any.at[:, 0], data.at[0:2]),
            (chg_any.at[:, 0], data.at[2:4]),
            (table_any, table),
        ],
        sems,
    )
    copies[0].wait()
    pos = pos_ref[...].astype(F32)
    order = sort_table(pos).astype(BF16)
    row = jnp.floor((pos + 0.5) * (1.0 / GRID))
    col = pos - row * GRID
    row = row + 8.0 * (jnp.where(row >= THIRD, 1.0, 0.0) + jnp.where(row >= 2 * THIRD, 1.0, 0.0))
    col = col + 8.0 * (jnp.where(col >= THIRD, 1.0, 0.0) + jnp.where(col >= 2 * THIRD, 1.0, 0.0))
    place = jnp.concatenate([row, col, jnp.zeros((SLOTS - 2, LANES), F32)], axis=0)
    high, low = halves(place)
    place = dot_t(high, order) + dot_t(low, order)
    for slot in range(4, SLOTS):
        line = place[slot - 4 : slot - 3, :]
        out_ref[pl.ds(slot, planes, stride=SLOTS), :] = jnp.broadcast_to(line, (planes, LANES))
    for copy in copies[1:]:
        copy.wait()
    both = jnp.concatenate(
        [
            data[0:2].reshape(2 * GRID, LANES),
            data[2:4].reshape(2 * GRID, LANES),
        ],
        axis=1,
    )
    high, low = halves(both)
    values = dot3(table[0], table[1], high, low)
    high, low = halves(jnp.concatenate([values[:, :LANES], values[:, LANES:]], axis=0))
    values = dot_t(high, order) + dot_t(low, order)
    for slot in range(4):
        out_ref[pl.ds(slot, planes, stride=SLOTS), :] = values[
            slot * planes : (slot + 1) * planes
        ]


def reorder_kernel(pot_ref, per_ref, order_ref, out_ref, done_ref, lines, rows):
    done_ref[0] = 0
    rows[...] = jnp.zeros_like(rows)
    lines[2 * GRID :, :] = jnp.zeros((GRID, LANES), F32)
    for field, ref in enumerate((pot_ref, per_ref)):
        for j in range(3):
            width = min(LANES, GRID - j * LANES)
            lines[j * GRID : (j + 1) * GRID, :width] = ref[0, :, j * LANES : j * LANES + width]
        for turn in range(3):
            for k in range(8):
                base = turn * LANES + 16 * k
                for j in range(3):
                    start = j * GRID + 45 * k + turn
                    rows[base : base + 15, j * LANES : (j + 1) * LANES] = lines[
                        pl.ds(start, 15, stride=3), :
                    ]
        high, low = halves(rows[...])
        out_ref[field] = dot(high, order_ref[...]) + dot(low, order_ref[...])


def exchange_lanes(blocks):
    group = lax.broadcasted_iota(jnp.int32, (SLOTS, LANES), 1) // GROUP
    blocks = list(blocks)
    for bit in range(4):
        step = 1 << bit
        high = (group & step) != 0
        for i in range(CHUNKS):
            if i & step:
                continue
            a, b = blocks[i], blocks[i + step]
            blocks[i] = jnp.where(high, pltpu.roll(b, GROUP * step, 1), a)
            blocks[i + step] = jnp.where(high, b, pltpu.roll(a, LANES - GROUP * step, 1))
    return blocks


def window_rows(vals, start, count):
    rows = lax.broadcasted_iota(jnp.int32, (count, WIDE), 0) + start
    return rows.astype(F32) == vals[4:5, :]


def column_hot(vals):
    cols = lax.broadcasted_iota(jnp.int32, (PAD, WIDE), 0).astype(F32)
    return jnp.where(cols == vals[5:6, :], 1.0, 0.0).astype(BF16)


def find_windows(group, win):
    most = 0
    for q in range(CHUNKS):
        rows = group[q * SLOTS + 4 : q * SLOTS + 5, :]
        low = jnp.min(rows).astype(jnp.int32)
        high = jnp.max(rows).astype(jnp.int32)
        start = jnp.bitwise_and(low, -16)
        more = lax.shift_right_logical(high - start + (WINDOW - FIRST[q]), 7)
        win[q] = start
        win[CHUNKS + q] = start + FIRST[q]
        win[2 * CHUNKS + q] = more
        most = jnp.maximum(most, more)
    return most


def over_windows(work, most, win):
    for q in range(CHUNKS):
        work(q, pl.multiple_of(win[q], 16), FIRST[q], True)

    @pl.when(most > 0)
    def _():
        def one(q, _):
            def block(b, _):
                work(q, pl.multiple_of(win[CHUNKS + q] + b * WINDOW, 16), WINDOW, False)
                return 0

            lax.fori_loop(0, win[2 * CHUNKS + q], block, 0)
            return 0

        lax.fori_loop(0, CHUNKS, one, 0)


def forward_kernel(
    done_ref, vals_ref, rh_ref, rl_ref, lh_ref, ll_ref,
    keep_ref, send_ref, real_ref, group_ref,
    win_ref, field, xh, xl, zh, zl, dens,
):
    core = lax.axis_index("band") % 2
    field[...] = jnp.zeros_like(field)
    for half in range(2):
        blocks = [
            vals_ref[(half * CHUNKS + j) * SLOTS : (half * CHUNKS + j + 1) * SLOTS, :]
            for j in range(CHUNKS)
        ]
        for q, block in enumerate(exchange_lanes(blocks)):
            group_ref[q * SLOTS : (q + 1) * SLOTS, half * LANES : (half + 1) * LANES] = block
    most = find_windows(group_ref, win_ref)

    def place(q, start, count, first):
        vals = group_ref[pl.ds(q * SLOTS if first else pl.multiple_of(q * SLOTS, SLOTS), SLOTS), :]
        hot = jnp.where(window_rows(vals, start, count), 1.0, 0.0).astype(BF16)
        cols = column_hot(vals)
        scaled = []
        for comp in range(4):
            high, low = halves(vals[comp : comp + 1, :])
            scaled.append(jnp.concatenate([hot * high, hot * low], axis=1))
        placed = lax.dot_general(
            jnp.concatenate(scaled, axis=0),
            jnp.concatenate([cols, cols], axis=1),
            (((1,), (1,)), ((), ())),
            preferred_element_type=F32,
        )
        for comp in range(4):
            field[comp, pl.ds(start, count), :] += placed[comp * count : (comp + 1) * count]

    over_windows(place, most, win_ref)

    step = 16
    for f in range(2):
        for r in range(0, LANES, step):
            rows = []
            for r2 in range(3):
                at = slice(r2 * LANES + r, r2 * LANES + r + step)
                cols = [
                    tuple(field[2 * f + k, at, c2 * LANES : (c2 + 1) * LANES] for k in range(2))
                    for c2 in range(3)
                ]
                rows.append(three_point(*cols, 1.0))
            for y2 in range(3):
                turned = three_point(rows[0][y2], rows[1][y2], rows[2][y2], 1.0)
                for x2 in range(3):
                    for k in range(2):
                        at = slice(f * PAD + x2 * LANES + r, f * PAD + x2 * LANES + r + step)
                        lanes = slice(y2 * WIDE + k * LANES, y2 * WIDE + (k + 1) * LANES)
                        high, low = halves(turned[x2][k])
                        xh[at, lanes] = high
                        xl[at, lanes] = low

    for y2 in range(3):
        at = slice(y2 * WIDE, (y2 + 1) * WIDE)
        out = dot3(xh[:, at], xl[:, at], rh_ref[at, :], rl_ref[at, :])
        for f in range(2):
            for x2 in range(3):
                for k in range(2):
                    part = out[
                        f * PAD + x2 * LANES : f * PAD + (x2 + 1) * LANES,
                        k * LANES : (k + 1) * LANES,
                    ]
                    rows = slice(x2 * WIDE + k * LANES, x2 * WIDE + (k + 1) * LANES)
                    lanes = slice(f * PAD + y2 * LANES, f * PAD + (y2 + 1) * LANES)
                    high, low = halves(part)
                    zh[rows, lanes] = high
                    zl[rows, lanes] = low

    for x2 in range(3):
        at = slice(x2 * WIDE, (x2 + 1) * WIDE)
        out = dot3(lh_ref[at, :], ll_ref[at, :], zh[at, :], zl[at, :])
        real_ref[at, :] = out
        dens[x2] = 2.0 * (out[:LANES, :PAD] * out[:LANES, PAD:] + out[LANES:, :PAD] * out[LANES:, PAD:])
        for m in range(4):
            own = pl.multiple_of(16 * (2 * m + core), 16)
            other = pl.multiple_of(16 * (2 * m + 1 - core), 16)
            keep_ref[m, 16 * x2 : 16 * (x2 + 1), :] = dens[x2, pl.ds(own, 16), :]
            send_ref[m, 16 * x2 : 16 * (x2 + 1), :] = dens[x2, pl.ds(other, 16), :]


def back_kernel(
    group_ref, real_ref, pot_ref, lh_ref, ll_ref, rh_ref, rl_ref, out_ref, done_ref,
    mid, ph, plow, grid, picked, win,
):
    done_ref[0] = 0
    grid[:, PAD:, :] = jnp.zeros((2, WINDOW, 2 * PAD), BF16)
    for x2 in range(3):
        at = slice(x2 * WIDE, (x2 + 1) * WIDE)
        rows = slice(x2 * LANES, (x2 + 1) * LANES)
        pot = jnp.concatenate([pot_ref[0, rows, :]] * 2, axis=0)
        per = jnp.concatenate([pot_ref[1, rows, :]] * 2, axis=0)
        high, low = halves(pot * real_ref[at, PAD:] + per * real_ref[at, :PAD])
        mid[at, :] = dot3(lh_ref[at, :], ll_ref[at, :], high, low)
    step = 16
    for r in range(0, LANES, step):
        for y2 in range(3):
            lanes = slice(y2 * LANES, (y2 + 1) * LANES)
            parts = [
                tuple(
                    mid[x2 * WIDE + k * LANES + r : x2 * WIDE + k * LANES + r + step, lanes]
                    for k in range(2)
                )
                for x2 in range(3)
            ]
            for r2, pair in enumerate(three_point(*parts, -1.0)):
                for k in range(2):
                    high, low = halves(pair[k])
                    rows = slice(r2 * LANES + r, r2 * LANES + r + step)
                    to = slice(y2 * WIDE + k * LANES, y2 * WIDE + (k + 1) * LANES)
                    ph[rows, to] = high
                    plow[rows, to] = low
    most = find_windows(group_ref, win)
    for y2 in range(3):
        at = slice(y2 * WIDE, (y2 + 1) * WIDE)
        out = dot3(ph[:, at], plow[:, at], rh_ref[at, :], rl_ref[at, :])
        mid[:PAD, y2 * LANES : (y2 + 1) * LANES] = out[:, :LANES]
        mid[PAD:, y2 * LANES : (y2 + 1) * LANES] = out[:, LANES:]
    for r in range(0, PAD, step):
        parts = [
            tuple(
                mid[k * PAD + r : k * PAD + r + step, y2 * LANES : (y2 + 1) * LANES]
                for k in range(2)
            )
            for y2 in range(3)
        ]
        for q2, pair in enumerate(three_point(*parts, -1.0)):
            for k in range(2):
                high, low = halves(pair[k])
                grid[k, r : r + step, q2 * LANES : (q2 + 1) * LANES] = high
                grid[k, r : r + step, PAD + q2 * LANES : PAD + (q2 + 1) * LANES] = low

    def pick(q, start, count, first):
        at = pl.ds(q * SLOTS if first else pl.multiple_of(q * SLOTS, SLOTS), SLOTS)
        vals = group_ref[at, :]
        mask = window_rows(vals, start, count)
        cols = column_hot(vals)
        lines = grid[:, pl.ds(start, count), :].reshape(2 * count, 2 * PAD)
        chosen = dot(lines, jnp.concatenate([cols, cols], axis=0))
        real = jnp.sum(jnp.where(mask, chosen[:count], 0.0), axis=0, keepdims=True)
        imag = jnp.sum(jnp.where(mask, chosen[count:], 0.0), axis=0, keepdims=True)
        found = jnp.concatenate([real, imag, jnp.zeros((SLOTS - 2, WIDE), F32)], axis=0)
        picked[at, :] = found if first else picked[at, :] + found

    over_windows(pick, most, win)
    for half in range(2):
        blocks = [
            picked[q * SLOTS : (q + 1) * SLOTS, half * LANES : (half + 1) * LANES]
            for q in range(CHUNKS)
        ]
        for j, block in enumerate(exchange_lanes(blocks)):
            src = half * CHUNKS + j
            out_ref[src * SLOTS : (src + 1) * SLOTS, :] = block


def pair_kernel(done_ref, keep_ref, got_ref, *rest):
    block_refs, total = rest[:4], rest[4]
    chip = lax.axis_index("band") // 2
    total[...] = keep_ref[...] + got_ref[...]
    for k in range(4):
        block_refs[k][...] = total[jnp.bitwise_xor(chip, k)]


def residual_kernel(
    pos_ref, table, order_ref, chg_ref, back_ref, energy_ref, *rest
):
    parts, (out_ref, dens_ref) = rest[:4], rest[4:]
    planes = back_ref.shape[0] // SLOTS
    lines = 2 * planes
    pos = pos_ref[...].astype(F32)
    order = sort_table(pos).astype(BF16)
    row = jnp.floor((pos + 0.5) * (1.0 / GRID))
    col = pos - row * GRID
    half = GRID // 2
    row = jnp.where(row < half, row, row - GRID)
    col = jnp.where(col < half, col, col - GRID)
    depth = lax.broadcasted_iota(jnp.int32, (GRID, LANES), 0).astype(F32)
    depth = jnp.where(depth < half, depth, depth - GRID)
    kinetic = (depth * depth + (row * row + col * col)) * (8.0 / (GRID * GRID))
    factor = kinetic - energy_ref[0]
    real = back_ref[pl.ds(0, planes, stride=SLOTS), :]
    imag = back_ref[pl.ds(1, planes, stride=SLOTS), :]
    high, low = halves(jnp.concatenate([real, imag], axis=0))
    both = dot(jnp.concatenate([high, low], axis=0), order).astype(BF16)
    applied = dot(table[...], jnp.concatenate([both, both[:lines]], axis=0))
    for k in range(2):
        out_ref[k, 0] = factor * chg_ref[k, 0] + applied[k * GRID : (k + 1) * GRID]
    high, low = halves(parts[0][...] + parts[1][...] + parts[2][...] + parts[3][...])
    total = dot_t(high, order_ref[...]) + dot_t(low, order_ref[...])
    for i in range(15):
        for x2 in range(3):
            dens_ref[3 * i + x2] = total[16 * x2 + i : 16 * x2 + i + 1, :GRID]


def in_vmem(count):
    return [pl.BlockSpec(memory_space=pltpu.VMEM)] * count


def in_hbm(count):
    return [pl.BlockSpec(memory_space=pltpu.HBM)] * count


def in_smem():
    return pl.BlockSpec(memory_space=pltpu.SMEM)


def call(kernel, name, outs, ins, out_specs, scratch=(), flops=0, limit=32):
    return pl.pallas_call(
        kernel,
        out_shape=outs,
        in_specs=ins,
        out_specs=out_specs,
        scratch_shapes=list(scratch),
        compiler_params=pltpu.CompilerParams(vmem_limit_bytes=limit * 1024 * 1024),
        cost_estimate=pl.CostEstimate(flops=flops, bytes_accessed=3_000_000, transcendentals=0),
        name=name,
    )


def shape(*dims, dtype=F32):
    return jax.ShapeDtypeStruct(dims, dtype)


def sems(count):
    return pltpu.SemaphoreType.DMA((count,))


def on_device(orbitals, response, potential, perturbation, energies, stick_pos):
    planes = lax.axis_size("pw")
    bands = lax.axis_size("band")
    cos, sin = trig(np.arange(planes), np.arange(GRID))
    to_planes = np.block([[cos, -sin], [sin, cos]]) / math.sqrt(GRID)
    to_planes = np.stack(split_table(to_planes))
    from_planes = np.block([[cos.T, sin.T], [-sin.T, cos.T]]) / math.sqrt(planes)
    high, low = split_table(from_planes)
    from_planes = np.concatenate([high, high, low], axis=1)
    right, left, left_back, right_back = transform_tables()
    order = column_order()
    pos = stick_pos.reshape(1, LANES)
    square = pltpu.VMEM((2 * PAD, 2 * PAD), BF16)
    grouped = pltpu.VMEM((CHUNKS * SLOTS, WIDE), F32)
    windows = pltpu.SMEM((3 * CHUNKS,), jnp.int32)

    packed = call(
        planes_kernel,
        "to_planes",
        shape(planes * SLOTS, LANES),
        in_hbm(4),
        in_vmem(1)[0],
        [
            pltpu.VMEM((1, LANES), jnp.int32),
            pltpu.VMEM(to_planes.shape, BF16),
            pltpu.VMEM((4, GRID, LANES), F32),
            sems(4),
        ],
        flops=500_000_000,
        limit=60,
    )(pos, to_planes, orbitals, response)
    arrived = lax.all_to_all(
        packed.reshape(planes, SLOTS, LANES), "pw", split_axis=0, concat_axis=0, tiled=True
    ).reshape(planes * SLOTS, LANES)
    pots, done = call(
        reorder_kernel,
        "reorder",
        [shape(2, PAD, PAD), shape(1, dtype=jnp.int32)],
        in_vmem(3),
        in_vmem(1) + [in_smem()],
        [pltpu.VMEM((3 * GRID, LANES), F32), pltpu.VMEM((PAD, PAD), F32)],
        flops=1_500_000_000,
        limit=60,
    )(potential, perturbation, order)

    keep, send, fields, group = call(
        forward_kernel,
        "place_and_transform",
        [
            shape(4, 48, PAD),
            shape(4, 48, PAD),
            shape(2 * PAD, 2 * PAD),
            shape(CHUNKS * SLOTS, WIDE),
        ],
        [in_smem()] + in_vmem(5),
        in_vmem(4),
        [windows, pltpu.VMEM((4, TALL, PAD), F32)]
        + [square] * 4
        + [pltpu.VMEM((3, LANES, PAD), F32)],
        flops=10_000_000_000,
    )(done, arrived, *right, *left)
    got = lax.ppermute(send, "band", [(i, i ^ 1) for i in range(bands)])
    picked, done = call(
        back_kernel,
        "back_and_pick",
        [shape(planes * SLOTS, LANES), shape(1, dtype=jnp.int32)],
        in_vmem(7),
        in_vmem(1) + [in_smem()],
        [
            pltpu.VMEM((2 * PAD, PAD), F32),
            pltpu.VMEM((PAD, 2 * PAD), BF16),
            pltpu.VMEM((PAD, 2 * PAD), BF16),
            pltpu.VMEM((2, TALL, 2 * PAD), BF16),
            grouped,
            windows,
        ],
        flops=6_000_000_000,
    )(group, fields, pots, *left_back, *right_back)
    returned = lax.all_to_all(
        picked.reshape(planes, SLOTS, LANES), "pw", split_axis=0, concat_axis=0, tiled=True
    ).reshape(planes * SLOTS, LANES)
    blocks = call(
        pair_kernel,
        "pair_sum",
        [shape(48, PAD)] * 4,
        [in_smem()] + in_vmem(2),
        in_vmem(4),
        [pltpu.VMEM((4, 48, PAD), F32)],
        flops=300_000,
    )(done, keep, got)
    parts = [blocks[0]] + [
        lax.ppermute(blocks[k], "band", [(i, i ^ (2 * k)) for i in range(bands)])
        for k in range(1, 4)
    ]

    residual, density = call(
        residual_kernel,
        "from_planes",
        [shape(2, 1, GRID, LANES), shape(GRID // bands, 1, GRID)],
        in_vmem(5) + [in_smem()] + in_vmem(4),
        in_vmem(2),
        flops=500_000_000,
    )(pos, from_planes, order, response, returned, energies, *parts)
    return (residual, density.reshape(1, GRID // bands, GRID))


def solution(mesh):
    placed = (
        P(None, "band", None, "pw"),
        P(None, "band", None, "pw"),
        P("pw", None, None),
        P("pw", None, None),
        P("band"),
        P("pw"),
    )
    return jax.shard_map(
        on_device,
        mesh=mesh,
        in_specs=placed,
        out_specs=(P(None, "band", None, "pw"), P("pw", "band", None)),
        check_vma=False,
    )
```
